128 devices in a mesh: row: 8 (over y_hi, z), col: 16 (over y_lo, x, core).
Axes of the slice: x: 4, y: 4 (y_hi: 2, y_lo: 2; y = y_hi * 2 + y_lo), z: 4, core: 2. Of those that a mesh axis runs over, the one named last changes fastest.
Arguments:
- transmission: float32 [2, 2, 2048, 8192], P(None, None, 'row', 'col'), may hold values from -1 to 1, as said below
- probe: float32 [2, 256, 256], replicated, may hold values from -6 to 6
- offsets: int32 [1024, 2], P(('row', 'col')), may hold values from 0 to 7936, as said below
- frames: int32 [1024, 256, 256], P(('row', 'col')), may hold values from 0 to 255
- lower_level: int32 [1024, 16, 16], P(('row', 'col')), may hold values from 0 to 7
- level_span: int32 [1024, 16, 16], P(('row', 'col')), may hold values from 0 to 15
Outputs:
- new_transmission: float32 [2, 2, 2048, 8192], P(None, None, 'row', 'col')
- new_probe: float32 [2, 256, 256], replicated
The draws below stay inside these ranges and needn't reach their ends.
Inputs may be any that keep to these rules, and one draw needn't show every extreme that they name: `transmission`: real and imaginary parts of complex transmissions of modulus below 1. `offsets`: A position's patch anchor lies in the tile of rows 256 and columns 512 of the device that holds the position, and the whole 256 x 256 patch lies inside the region.
All inputs are finite; a program needn't handle non-finite values.
Results may differ from the reference program's by a relative error of at most 0.0003.
Values sent between devices are 32-bit elements; how exact they have to be, the bound alone decides.
A program may use at most 192 MiB of HBM per device.

```python
import math
import jax
import jax.numpy as jnp
from jax import lax

P_SIZE = 256
SLICES = 2
NBK = 16
TR = 256
TC = 512
POS_DEV = 8
NY = 2048
NX = 8192
NPOS = 1024
N_ROW = 8
N_COL = 16


def draw_transmission(key, part):
    key = jax.random.fold_in(key, 11)
    first, second = jax.random.split(key)
    amplitude = jax.random.uniform(first, (SLICES, NY, NX), jnp.float32, 0.5, 0.999)
    phase = jax.random.uniform(second, (SLICES, NY, NX), jnp.float32, -1.0, 1.0)
    return jnp.stack([amplitude * jnp.cos(phase), amplitude * jnp.sin(phase)], 1)


def draw_offsets(key, part):
    key = jax.random.fold_in(key, 23)
    first, second = jax.random.split(key)
    number = jnp.arange(NPOS, dtype=jnp.int32)
    owner = number // POS_DEV
    within = number % POS_DEV
    row_owner = owner // N_COL
    col_owner = owner % N_COL
    row_step = jax.random.randint(first, (NPOS,), 0, TR, dtype=jnp.int32)
    col_step = jax.random.randint(second, (NPOS,), 0, TC, dtype=jnp.int32)
    lowest = (owner == 0) & (within == 0)
    highest = (owner == N_ROW * N_COL - 1) & (within == POS_DEV - 1)
    row_step = jnp.where(lowest, 0, jnp.where(highest, TR - 1, row_step))
    col_step = jnp.where(lowest, 0, jnp.where(highest, TC - 1, col_step))
    row_place = jnp.minimum(row_owner * TR + row_step, NY - P_SIZE)
    col_place = jnp.minimum(col_owner * TC + col_step, NX - P_SIZE)
    return jnp.stack([row_place, col_place], 1).astype(jnp.int32)


def place_ends(array, key, smallest, top_value):
    longest = array.shape.index(max(array.shape))
    spots = []
    for shift in (0, 1):
        where = [jax.random.randint(jax.random.fold_in(key, axis), (), 0, length) for axis, length in enumerate(array.shape)]
        where[longest] = (where[longest] + shift) % array.shape[longest]
        spots.append(tuple(where))
    return array.at[spots[0]].set(smallest).at[spots[1]].set(top_value)


def normal_values(rng, shape, deviation, reach, kind=jnp.bfloat16):
    drawn = deviation * jax.random.normal(rng, shape, jnp.float32)
    return jnp.clip(drawn, min=-reach, max=reach).astype(kind)


def setup_inputs(seed: int = 0) -> dict:
    seeds = jax.random.split(jax.random.key(seed), 7)
    return {
        "transmission": draw_transmission(jax.random.fold_in(seeds[6], 71), 0),
        "probe": normal_values(seeds[1], (2, P_SIZE, P_SIZE), 1.0, 6.0, jnp.float32),
        "offsets": draw_offsets(jax.random.fold_in(seeds[6], 71), 0),
        "frames": place_ends(jax.random.randint(seeds[3], (NPOS, P_SIZE, P_SIZE), 0, 256), jax.random.fold_in(seeds[3], 1), 0, 255).astype(jnp.int32),
        "lower_level": place_ends(jax.random.randint(seeds[4], (NPOS, NBK, NBK), 0, 8), jax.random.fold_in(seeds[4], 1), 0, 7).astype(jnp.int32),
        "level_span": place_ends(jax.random.randint(seeds[5], (NPOS, NBK, NBK), 0, 16), jax.random.fold_in(seeds[5], 1), 0, 15).astype(jnp.int32),
    }


PROPAGATION = 0.5
OBJECT_RATE = 0.1
PROBE_RATE = 0.5

def kernel_parts(size):
    freq = jnp.arange(size, dtype=jnp.int32)
    freq = jnp.where(freq < size // 2, freq, freq - size)
    square = freq * freq
    total = square[:, None] + square[None, :]
    phase = total.astype(jnp.float32) * (-PROPAGATION * math.pi / size)
    return (jnp.cos(phase), jnp.sin(phase))

def intensity(counts, lower, span):
    blocks = lower.shape[-1]
    block = counts.shape[-1] // blocks
    base = 0.02 * jnp.exp2(lower.astype(jnp.float32) * 0.25)
    extent = 0.1 * jnp.exp2(span.astype(jnp.float32) * 0.25)
    shaped = counts.astype(jnp.float32).reshape(counts.shape[:-2] + (blocks, block, blocks, block))
    value = base[..., :, None, :, None] + shaped * (extent[..., :, None, :, None] / 255.0)
    return value.reshape(counts.shape)

def reference(transmission, probe, offsets, frames, lower_level, level_span):
    cos_part, sin_part = kernel_parts(P_SIZE)
    kernel = cos_part + 1j * sin_part
    field = transmission[:, 0] + 1j * transmission[:, 1]
    wave = probe[0] + 1j * probe[1]

    def forward_prop(values):
        return jnp.fft.ifft2(kernel * jnp.fft.fft2(values, norm='ortho'), norm='ortho')

    def adjoint_prop(values):
        return jnp.fft.ifft2(jnp.conj(kernel) * jnp.fft.fft2(values, norm='ortho'), norm='ortho')

    def one_position(carry, inputs):
        grad_field, grad_wave = carry
        place, counts, lower, span = inputs
        start = (jnp.int32(0), place[0].astype(jnp.int32), place[1].astype(jnp.int32))
        patches = lax.dynamic_slice(field, start, (SLICES, P_SIZE, P_SIZE))
        incoming = []
        current = wave
        for layer in range(SLICES):
            incoming.append(current)
            current = current * patches[layer]
            if layer < SLICES - 1:
                current = forward_prop(current)
        far = jnp.fft.fft2(current, norm='ortho')
        measured = intensity(counts, lower, span)
        misfit = far.real * far.real + far.imag * far.imag - measured
        back = jnp.fft.ifft2(misfit * far, norm='ortho')
        pieces = [None] * SLICES
        for layer in reversed(range(SLICES)):
            pieces[layer] = back * jnp.conj(incoming[layer])
            back = back * jnp.conj(patches[layer])
            if layer > 0:
                back = adjoint_prop(back)
        stacked = jnp.stack(pieces)
        grad_field = lax.dynamic_update_slice(grad_field, lax.dynamic_slice(grad_field, start, (SLICES, P_SIZE, P_SIZE)) + stacked, start)
        return ((grad_field, grad_wave + back), None)
    initial = (jnp.zeros_like(field), jnp.zeros_like(wave))
    (grad_field, grad_wave), unused = lax.scan(one_position, initial, (offsets, frames, lower_level, level_span))
    step_field = jnp.stack([grad_field.real, grad_field.imag], 1)
    step_wave = jnp.stack([grad_wave.real, grad_wave.imag])
    new_transmission = transmission - OBJECT_RATE * step_field
    new_probe = probe - PROBE_RATE / math.sqrt(NPOS) * step_wave
    return (new_transmission.astype(jnp.float32), new_probe.astype(jnp.float32))
```

```python
import functools
import math

import jax
import jax.numpy as jnp
import numpy as np
from jax import lax
from jax.experimental import pallas as pl
from jax.experimental.pallas import tpu as pltpu
from jax.sharding import PartitionSpec as P

PROPAGATION = 0.5
OBJECT_RATE = 0.1
PROBE_RATE = 0.5
N = 256
HALF = 128
NBK = 16
DIMS = dict(yh=2, z=4, yl=2, x=4, core=2)
MESH = pl.DeviceIdType.MESH
F32 = jnp.float32
BF16 = jnp.bfloat16


def block_pairs():
    n = np.arange(N)
    dft = np.exp(-2j * np.pi * np.outer(n, n) / N) / math.sqrt(N)
    freq = np.where(n < HALF, n, n - N).astype(np.float64)
    chirp = np.exp(-1j * np.pi * PROPAGATION * freq * freq / N)
    prop = dft.conj().T @ (chirp[:, None] * dft)
    fu, fv = dft[0::2, :HALF], dft[1::2, :HALF]
    first, second = prop[:HALF, :HALF], prop[:HALF, HALF:]
    cu, cv = (first + second) / 2, (first - second) / 2
    return {
        "prop": (cu, cv),
        "dft": (fu, fv),
        "idft": (fu.conj().T, fv.conj().T),
        "adj": (cu.conj().T, cv.conj().T),
    }


ORDER = ("prop", "dft", "idft", "adj")


def tables():
    left, right = [], []
    pairs = block_pairs()
    for name in ORDER:
        for m in pairs[name]:
            real = np.block([[m.real, -m.imag], [m.imag, m.real]]).astype(np.float32)
            hi = np.asarray(real, dtype=jnp.bfloat16)
            lo = np.asarray(real - hi.astype(np.float32), dtype=jnp.bfloat16)
            left.append(np.concatenate([hi, hi, lo], 1))
            right.append(np.concatenate([hi.T, hi.T, lo.T], 0))
    return np.stack(left), np.stack(right)


def permutation():
    perm = np.zeros((N, N), np.float32)
    for p in range(N):
        perm[p, 2 * p if p < HALF else 2 * (p - HALF) + 1] = 1
    rows = np.asarray(perm, dtype=jnp.bfloat16)
    cols = np.asarray(perm.T, dtype=jnp.bfloat16)
    spread = np.zeros((NBK, N), np.float32)
    for p in range(N):
        spread[(p % HALF) // 8, p] = 1
    return rows, cols, spread


def split(x):
    hi = x.astype(BF16)
    lo = (x - hi.astype(F32)).astype(BF16)
    return hi, lo


def dot(a, b):
    return jnp.dot(a, b, preferred_element_type=F32)


def along_cols(re, im, right_ref, op, pre, post):
    a, b, c, d = re[:, :HALF], re[:, HALF:], im[:, :HALF], im[:, HALF:]
    if pre:
        u = jnp.concatenate([a + b, c + d], 1)
        v = jnp.concatenate([a - b, c - d], 1)
    else:
        u = jnp.concatenate([a, c], 1)
        v = jnp.concatenate([b, d], 1)
    out = []
    for i, x in enumerate((u, v)):
        hi, lo = split(x)
        out.append(dot(jnp.concatenate([hi, lo, hi], 1), right_ref[2 * op + i]))
    yu, yv = out
    if post:
        p, m = yu + yv, yu - yv
    else:
        p, m = yu, yv
    return (
        jnp.concatenate([p[:, :HALF], m[:, :HALF]], 1),
        jnp.concatenate([p[:, HALF:], m[:, HALF:]], 1),
    )


def along_rows(re, im, left_ref, op, pre, post):
    a, b, c, d = re[:HALF], re[HALF:], im[:HALF], im[HALF:]
    if pre:
        u = jnp.concatenate([a + b, c + d], 0)
        v = jnp.concatenate([a - b, c - d], 0)
    else:
        u = jnp.concatenate([a, c], 0)
        v = jnp.concatenate([b, d], 0)
    out = []
    for i, x in enumerate((u, v)):
        hi, lo = split(x)
        out.append(dot(left_ref[2 * op + i], jnp.concatenate([hi, lo, hi], 0)))
    yu, yv = out
    if post:
        p, m = yu + yv, yu - yv
    else:
        p, m = yu, yv
    return (
        jnp.concatenate([p[:HALF], m[:HALF]], 0),
        jnp.concatenate([p[HALF:], m[HALF:]], 0),
    )


def transform(re, im, left_ref, right_ref, op, pre, post):
    re, im = along_cols(re, im, right_ref, op, pre, post)
    return along_rows(re, im, left_ref, op, pre, post)


def complex_mul(a, b):
    return a[0] * b[0] - a[1] * b[1], a[0] * b[1] + a[1] * b[0]


def conj_mul(a, b):
    return a[0] * b[0] + a[1] * b[1], a[1] * b[0] - a[0] * b[1]


def kernel(
    batch,
    rate,
    dims,
    place_ref,
    trans_hbm,
    probe_ref,
    frames_hbm,
    lower_ref,
    span_ref,
    left_hbm,
    right_hbm,
    perm_rows_ref,
    perm_cols_ref,
    spread_ref,
    grad_ref,
    newprobe_ref,
    own0,
    own1,
    bel0,
    bel1,
    gown0,
    gown1,
    gbel0,
    gbel1,
    rin0,
    rin1,
    din0,
    din1,
    frames,
    left,
    right,
    meas,
    wav,
    patch0,
    amp,
    piece,
    gacc,
    stage_core,
    stage_x,
    stage_y,
    stage_z,
    local_sem,
    send_sem,
    recv_sem,
):
    own, bel = (own0, own1), (bel0, bel1)
    gown, gbel = (gown0, gown1), (gbel0, gbel1)
    rin, din = (rin0, rin1), (din0, din1)
    n_z, n_x, n_yl, n_yh = dims["z"], dims["x"], dims["yl"], dims["yh"]
    n_row, n_col = n_yh * n_z, n_yl * n_x * 2
    row, col = lax.axis_index("row"), lax.axis_index("col")
    yh, z = row // n_z, row % n_z
    yl, x, core = col // (2 * n_x), (col // 2) % n_x, col % 2
    y_digit = yh * n_yl + yl
    n_y = n_yh * n_yl

    has_up, has_down = row > 0, row < n_row - 1
    has_left, has_right = col > 0, col < n_col - 1
    up, down = (row - 1, col), (row + 1, col)
    lft, rgt = (row, col - 1), (row, col + 1)

    def core_member(m):
        return (row, yl * 2 * n_x + x * 2 + m)

    def x_member(m):
        return (row, yl * 2 * n_x + m * 2 + core)

    def y_member(m):
        return ((m // n_yl) * n_z + z, (m % n_yl) * 2 * n_x + x * 2 + core)

    def z_member(m):
        return (yh * n_z + m, col)

    def load(src, dst, i):
        return pltpu.make_async_copy(src, dst, local_sem.at[i])

    loads = []
    for s in range(2):
        for c in range(2):
            loads.append(
                load(trans_hbm.at[s, :, :, pl.ds(c * N, N)], own[s].at[c], 2 * s + c)
            )
    loads.append(load(frames_hbm, frames, 4))
    loads.append(load(left_hbm, left, 5))
    loads.append(load(right_hbm, right, 6))
    for c in loads:
        c.start()

    barrier = pltpu.get_barrier_semaphore()

    def hail(dev):
        pl.semaphore_signal(barrier, inc=1, device_id=dev, device_id_type=MESH)

    for cond, dev in (
        (has_up, up),
        (has_down, down),
        (has_left, lft),
        (has_right, rgt),
    ):

        @pl.when(cond)
        def _(dev=dev):
            hail(dev)

    groups = (
        (core_member, 2, core),
        (x_member, n_x, x),
        (y_member, n_y, y_digit),
        (z_member, n_z, z),
    )
    for member, size, me in groups:
        for k in range(1, size):
            hail(member((me + k) % size))
    hails = sum(size - 1 for _, size, _ in groups)
    for cond in (has_up, has_down, has_left, has_right):
        hails = hails + jnp.where(cond, 1, 0)
    pl.semaphore_wait(barrier, hails)

    def remote(src, dst, i, dev):
        return pltpu.make_async_remote_copy(
            src_ref=src,
            dst_ref=dst,
            send_sem=send_sem.at[i],
            recv_sem=recv_sem.at[i],
            device_id=dev,
            device_id_type=MESH,
        )

    def fwd_rows(s, c):
        return remote(
            trans_hbm.at[s, :, :, pl.ds(c * N, N)], bel[s].at[c], 8 * s + c, up
        )

    def fwd_side(s):
        return remote(trans_hbm.at[s, :, :, pl.ds(0, N)], own[s].at[2], 8 * s + 2, lft)

    def fwd_corner(s):
        return remote(bel[s].at[0], bel[s].at[2], 8 * s + 3, lft)

    def back_corner(s):
        return remote(gbel[s].at[2], rin[s].at[1], 8 * s + 4, rgt)

    def back_side(s):
        return remote(gown[s].at[2], rin[s].at[0], 8 * s + 5, rgt)

    def back_rows(s, c):
        return remote(gbel[s].at[c], din[s].at[c], 8 * s + 6 + c, down)

    def on(cond, f):
        @pl.when(cond)
        def _():
            f()

    for c in range(2):
        on(has_up, fwd_rows(0, c).start)
    on(has_left, fwd_side(0).start)

    zero3 = jnp.zeros((2, N, N), F32)
    for s in range(2):

        @pl.when(jnp.logical_not(has_down))
        def _(s=s):
            for c in range(3):
                bel[s][c] = zero3

        @pl.when(jnp.logical_not(has_right))
        def _(s=s):
            own[s][2] = zero3
            on(has_down, functools.partial(bel[s].__setitem__, 2, zero3))

        @pl.when(jnp.logical_not(has_up))
        def _(s=s):
            for c in range(2):
                din[s][c] = zero3

        @pl.when(jnp.logical_not(has_left))
        def _(s=s):
            for c in range(2):
                rin[s][c] = zero3

    loads[4].wait()
    for c in loads[5:]:
        c.wait()

    def place(j):
        return place_ref[2 * j], place_ref[2 * j + 1]

    @pl.loop(0, batch)
    def _(j):
        counts = frames[j].astype(F32).astype(BF16)
        mixed = dot(perm_rows_ref[...], counts).astype(BF16)
        counts = dot(mixed, perm_cols_ref[...])
        base = 0.02 * jnp.exp2(lower_ref[j].astype(F32) * 0.25)
        extent = (0.1 / 255.0) * jnp.exp2(span_ref[j].astype(F32) * 0.25)

        def widen(small):
            wide = jnp.dot(
                small,
                spread_ref[...],
                precision=lax.Precision.HIGHEST,
                preferred_element_type=F32,
            )
            tall = jnp.broadcast_to(wide[:, None, :], (NBK, 8, N)).reshape(HALF, N)
            return jnp.concatenate([tall, tall], 0)

        meas[j] = widen(base) + counts * widen(extent)
        y, x = place(j)
        shift = x % N
        for p in range(2):
            wav[j, p] = pltpu.roll(pltpu.roll(probe_ref[p], shift, 1), y, 0)

    def masks(j):
        y, x = place(j)
        rows = lax.broadcasted_iota(jnp.int32, (N, N), 0) >= y
        cols = lax.broadcasted_iota(jnp.int32, (N, N), 1) >= x % N
        return rows, cols, x // N

    def take(s, j, p):
        rows, cols, k = masks(j)
        here = jnp.where(cols, own[s][k, p], own[s][k + 1, p])
        below = jnp.where(cols, bel[s][k, p], bel[s][k + 1, p])
        return jnp.where(rows, here, below)

    def arrive(s):
        @pl.when(has_down)
        def _():
            fwd_rows(s, 0).wait_recv()

        @pl.when(jnp.logical_and(has_down, has_left))
        def _():
            fwd_corner(s).start()

        if s == 0:
            for c in range(2):
                on(has_up, fwd_rows(1, c).start)
            on(has_left, fwd_side(1).start)

        @pl.when(has_down)
        def _():
            fwd_rows(s, 1).wait_recv()

        @pl.when(has_right)
        def _():
            fwd_side(s).wait_recv()

        @pl.when(jnp.logical_and(has_down, has_right))
        def _():
            fwd_corner(s).wait_recv()

    for c in loads[:4]:
        c.wait()
    arrive(0)

    @pl.loop(0, batch)
    def _(j):
        patch = take(0, j, 0), take(0, j, 1)
        patch0[j, 0], patch0[j, 1] = patch
        wave = complex_mul((wav[j, 0], wav[j, 1]), patch)
        amp[j, 0], amp[j, 1] = transform(*wave, left, right, 0, True, True)

    arrive(1)

    @pl.loop(0, batch)
    def _(j):
        patch = take(1, j, 0), take(1, j, 1)
        incoming = amp[j, 0], amp[j, 1]
        far = transform(*complex_mul(incoming, patch), left, right, 1, True, False)
        misfit = far[0] * far[0] + far[1] * far[1] - meas[j]
        back = transform(misfit * far[0], misfit * far[1], left, right, 2, False, True)
        piece[j, 0], piece[j, 1] = conj_mul(back, incoming)
        amp[j, 0], amp[j, 1] = conj_mul(back, patch)

    def accumulate(s):
        @pl.loop(0, N // 8)
        def _(i):
            here = pl.ds(pl.multiple_of(i * 8, 8), 8)
            rows = lax.broadcasted_iota(jnp.int32, (8, N), 0) + i * 8
            cols = lax.broadcasted_iota(jnp.int32, (8, N), 1)
            for p in range(2):
                sums = [[jnp.zeros((8, N), F32) for _ in range(3)] for _ in range(2)]
                for j in range(batch):
                    y, x = place(j)
                    value = piece[j, p, here, :]
                    target = x // N + jnp.where(cols >= x % N, 0, 1)
                    upper = jnp.where(rows >= y, value, 0.0)
                    for r, part in enumerate((upper, value - upper)):
                        for c in range(3):
                            sums[r][c] += jnp.where(target == c, part, 0.0)
                for c in range(3):
                    gown[s][c, p, here, :] = sums[0][c]
                    gbel[s][c, p, here, :] = sums[1][c]

    def send_back(s):
        on(has_right, back_corner(s).start)
        on(has_down, back_rows(s, 1).start)
        on(has_right, back_side(s).start)

    def send_back_late(s):
        @pl.when(has_left)
        def _():
            back_corner(s).wait_recv()

        gbel[s][0] += rin[s][1]
        on(has_down, back_rows(s, 0).start)

    accumulate(1)
    send_back(1)
    send_back_late(1)

    gacc[...] = jnp.zeros_like(gacc)

    @pl.loop(0, batch)
    def _(j):
        back = transform(amp[j, 0], amp[j, 1], left, right, 3, True, True)
        piece[j, 0], piece[j, 1] = conj_mul(back, (wav[j, 0], wav[j, 1]))
        term = conj_mul(back, (patch0[j, 0], patch0[j, 1]))
        y, x = place(j)
        for p in range(2):
            turned = pltpu.roll(pltpu.roll(term[p], (N - y) % N, 0), (N - x % N) % N, 1)
            for h in range(2):
                gacc[pl.ds((2 * p + h) * N, N), :] += turned[:, h * HALF : (h + 1) * HALF]

    accumulate(0)
    send_back(0)
    send_back_late(0)

    total = gacc.shape[0]
    stages = (
        (stage_core, core_member, 2, core, 16),
        (stage_x, x_member, n_x, x, 18),
        (stage_y, y_member, n_y, y_digit, 22),
        (stage_z, z_member, n_z, z, 26),
    )
    length = total
    base = 0
    spans = []
    for stage, member, size, me, sem in stages:
        chunk = length // size
        copies = []
        for k in range(1, size):
            m = (me + k) % size
            src = gacc.at[pl.ds(pl.multiple_of(base + m * chunk, 8), chunk), :]
            copies.append(remote(src, stage.at[k - 1], sem + k - 1, member(m)))
        for c in copies:
            c.start()
        spans.append((base, length, chunk))
        base = base + me * chunk
        mine = pl.ds(pl.multiple_of(base, 8), chunk)
        for c in copies:
            c.wait()
        got = gacc[mine, :]
        for k in range(1, size):
            got = got + stage[k - 1]
        gacc[mine, :] = got
        length = chunk

    mine = pl.ds(pl.multiple_of(base, 8), length)
    newprobe_ref[mine, :] = gacc[mine, :]
    for (stage, member, size, me, sem), (start, length, chunk) in reversed(
        list(zip(stages, spans))
    ):
        held = newprobe_ref.at[pl.ds(pl.multiple_of(start + me * chunk, 8), chunk), :]
        copies = [
            remote(held, held, 14 + sem + k - 1, member((me + k) % size))
            for k in range(1, size)
        ]
        for c in copies:
            c.start()
        for k, c in enumerate(copies, 1):
            c.wait_send()
            m = (me - k + size) % size
            there = newprobe_ref.at[pl.ds(pl.multiple_of(start + m * chunk, 8), chunk), :]
            remote(there, there, 14 + sem + k - 1, member(m)).wait_recv()

    for s in (1, 0):

        @pl.when(has_left)
        def _(s=s):
            back_side(s).wait_recv()

        for c in range(2):

            @pl.when(has_up)
            def _(s=s, c=c):
                back_rows(s, c).wait_recv()

            for p in range(2):
                value = gown[s][c, p] + din[s][c, p]
                if c == 0:
                    value = value + rin[s][0, p]
                grad_ref[s, p, :, pl.ds(c * N, N)] = value

    for s in range(2):
        for c in range(2):
            on(has_up, fwd_rows(s, c).wait_send)
            on(has_down, back_rows(s, c).wait_send)
        on(has_left, fwd_side(s).wait_send)
        on(jnp.logical_and(has_down, has_left), fwd_corner(s).wait_send)
        on(has_right, back_corner(s).wait_send)
        on(has_right, back_side(s).wait_send)


def body(dims, transmission, probe, offsets, frames, lower_level, level_span):
    batch = offsets.shape[0]
    layers, _, rows, cols = transmission.shape
    anchor = jnp.stack([lax.axis_index("row") * rows, lax.axis_index("col") * cols])
    place = (offsets - anchor[None, :]).reshape(2 * batch)
    left, right = tables()
    perm_rows, perm_cols, spread = permutation()
    n_y = dims["yh"] * dims["yl"]
    total = 2 * 2 * N
    chunk_core = total // 2
    chunk_x = chunk_core // dims["x"]
    chunk_y = chunk_x // n_y
    chunk_z = chunk_y // dims["z"]
    count_all = batch * lax.axis_size("row") * lax.axis_size("col")
    rate = PROBE_RATE / math.sqrt(count_all)
    any_space = pl.BlockSpec(memory_space=pl.ANY)
    vmem = pl.BlockSpec(memory_space=pltpu.VMEM)
    smem = pl.BlockSpec(memory_space=pltpu.SMEM)

    def block(*shape, dtype=F32):
        return pltpu.VMEM(shape, dtype)

    tile = [block(3, 2, N, N) for _ in range(8)]
    arriving = [block(2, 2, N, N) for _ in range(4)]
    scratch = (
        tile
        + arriving
        + [
            block(batch, N, N, dtype=jnp.int32),
            block(8, N, 3 * N, dtype=BF16),
            block(8, 3 * N, N, dtype=BF16),
            block(batch, N, N),
            block(batch, 2, N, N),
            block(batch, 2, N, N),
            block(batch, 2, N, N),
            block(batch, 2, N, N),
            block(total, HALF),
            block(1, chunk_core, HALF),
            block(max(dims["x"] - 1, 1), chunk_x, HALF),
            block(max(n_y - 1, 1), chunk_y, HALF),
            block(max(dims["z"] - 1, 1), chunk_z, HALF),
            pltpu.SemaphoreType.DMA((7,)),
            pltpu.SemaphoreType.DMA((48,)),
            pltpu.SemaphoreType.DMA((48,)),
        ]
    )
    gradient, probe_sum = pl.pallas_call(
        functools.partial(kernel, batch, rate, dims),
        out_shape=(
            jax.ShapeDtypeStruct(transmission.shape, F32),
            jax.ShapeDtypeStruct((total, HALF), F32),
        ),
        in_specs=[smem, any_space, vmem, any_space, vmem, vmem, any_space, any_space]
        + [vmem] * 3,
        out_specs=(vmem, vmem),
        scratch_shapes=scratch,
        compiler_params=pltpu.CompilerParams(
            collective_id=0, has_side_effects=True, vmem_limit_bytes=62 * 2**20
        ),
        name="ptycho_step",
    )(
        place,
        transmission,
        probe,
        frames,
        lower_level,
        level_span,
        left,
        right,
        perm_rows,
        perm_cols,
        spread,
    )
    summed = probe_sum.reshape(2, 2, N, HALF).transpose(0, 2, 1, 3).reshape(2, N, N)
    return transmission - OBJECT_RATE * gradient, probe - rate * summed


def solution(mesh):
    in_specs = (
        P(None, None, "row", "col"),
        P(),
        P(("row", "col"), None),
        P(("row", "col"), None, None),
        P(("row", "col"), None, None),
        P(("row", "col"), None, None),
    )
    out_specs = (P(None, None, "row", "col"), P())
    return jax.shard_map(
        functools.partial(body, DIMS),
        mesh=mesh,
        in_specs=in_specs,
        out_specs=out_specs,
        check_vma=False,
    )
```

```python
import functools
import math

import jax
import jax.numpy as jnp
import numpy as np
from jax import lax
from jax.experimental import pallas as pl
from jax.experimental.pallas import tpu as pltpu
from jax.sharding import PartitionSpec as P

PROPAGATION = 0.5
OBJECT_RATE = 0.1
PROBE_RATE = 0.5
N = 256
HALF = 128
NBK = 16
DIMS = dict(yh=2, z=4, yl=2, x=4, core=2)
MESH = pl.DeviceIdType.MESH
PIECES = ((0, 0, 256, False), (1, 0, 160, True))
LONG = (1, 160, 96)
N_SEMS = 64
F32 = jnp.float32
BF16 = jnp.bfloat16


def block_pairs():
    n = np.arange(N)
    dft = np.exp(-2j * np.pi * np.outer(n, n) / N) / math.sqrt(N)
    freq = np.where(n < HALF, n, n - N).astype(np.float64)
    chirp = np.exp(-1j * np.pi * PROPAGATION * freq * freq / N)
    prop = dft.conj().T @ (chirp[:, None] * dft)
    fu, fv = dft[0::2, :HALF], dft[1::2, :HALF]
    first, second = prop[:HALF, :HALF], prop[:HALF, HALF:]
    cu, cv = (first + second) / 2, (first - second) / 2
    return {
        "prop": (cu, cv),
        "dft": (fu, fv),
        "idft": (fu.conj().T, fv.conj().T),
        "adj": (cu.conj().T, cv.conj().T),
    }


ORDER = ("prop", "dft", "idft", "adj")


def tables():
    left, right = [], []
    pairs = block_pairs()
    for name in ORDER:
        for m in pairs[name]:
            real = np.block([[m.real, -m.imag], [m.imag, m.real]]).astype(np.float32)
            hi = np.asarray(real, dtype=jnp.bfloat16)
            lo = np.asarray(real - hi.astype(np.float32), dtype=jnp.bfloat16)
            left.append(np.concatenate([hi, hi, lo], 1))
            right.append(np.concatenate([hi.T, hi.T, lo.T], 0))
    return np.stack(left), np.stack(right)


def permutation():
    perm = np.zeros((N, N), np.float32)
    for p in range(N):
        perm[p, 2 * p if p < HALF else 2 * (p - HALF) + 1] = 1
    rows = np.asarray(perm, dtype=jnp.bfloat16)
    cols = np.asarray(perm.T, dtype=jnp.bfloat16)
    spread = np.zeros((NBK, N), np.float32)
    for p in range(N):
        spread[(p % HALF) // 8, p] = 1
    return rows, cols, spread


def split(x):
    hi = x.astype(BF16)
    lo = (x - hi.astype(F32)).astype(BF16)
    return hi, lo


def dot(a, b):
    return jnp.dot(a, b, preferred_element_type=F32)


def along_cols(re, im, right_ref, op, pre, post):
    a, b, c, d = re[:, :HALF], re[:, HALF:], im[:, :HALF], im[:, HALF:]
    if pre:
        u = jnp.concatenate([a + b, c + d], 1)
        v = jnp.concatenate([a - b, c - d], 1)
    else:
        u = jnp.concatenate([a, c], 1)
        v = jnp.concatenate([b, d], 1)
    out = []
    for i, x in enumerate((u, v)):
        hi, lo = split(x)
        out.append(dot(jnp.concatenate([hi, lo, hi], 1), right_ref[2 * op + i]))
    yu, yv = out
    if post:
        p, m = yu + yv, yu - yv
    else:
        p, m = yu, yv
    return (
        jnp.concatenate([p[:, :HALF], m[:, :HALF]], 1),
        jnp.concatenate([p[:, HALF:], m[:, HALF:]], 1),
    )


def along_rows(re, im, left_ref, op, pre, post):
    a, b, c, d = re[:HALF], re[HALF:], im[:HALF], im[HALF:]
    if pre:
        u = jnp.concatenate([a + b, c + d], 0)
        v = jnp.concatenate([a - b, c - d], 0)
    else:
        u = jnp.concatenate([a, c], 0)
        v = jnp.concatenate([b, d], 0)
    out = []
    for i, x in enumerate((u, v)):
        hi, lo = split(x)
        out.append(dot(left_ref[2 * op + i], jnp.concatenate([hi, lo, hi], 0)))
    yu, yv = out
    if post:
        p, m = yu + yv, yu - yv
    else:
        p, m = yu, yv
    return (
        jnp.concatenate([p[:HALF], m[:HALF]], 0),
        jnp.concatenate([p[HALF:], m[HALF:]], 0),
    )


def transform(re, im, left_ref, right_ref, op, pre, post):
    re, im = along_cols(re, im, right_ref, op, pre, post)
    return along_rows(re, im, left_ref, op, pre, post)


def complex_mul(a, b):
    return a[0] * b[0] - a[1] * b[1], a[0] * b[1] + a[1] * b[0]


def conj_mul(a, b):
    return a[0] * b[0] + a[1] * b[1], a[1] * b[0] - a[0] * b[1]


def kernel(
    batch,
    rate,
    dims,
    place_ref,
    trans_hbm,
    probe_ref,
    frames_hbm,
    lower_ref,
    span_ref,
    left_hbm,
    right_hbm,
    perm_rows_ref,
    perm_cols_ref,
    spread_ref,
    grad_ref,
    newprobe_ref,
    own0,
    own1,
    bel0,
    bel1,
    gown0,
    gown1,
    gbel0,
    gbel1,
    rin0,
    rin1,
    din0,
    din1,
    relay_up,
    relay_down,
    long_up,
    long_down,
    side_mid,
    frames,
    left,
    right,
    meas,
    wav,
    patch0,
    amp,
    piece,
    gacc,
    stage_core,
    stage_x,
    stage_y,
    stage_z,
    local_sem,
    send_sem,
    recv_sem,
):
    own, bel = (own0, own1), (bel0, bel1)
    gown, gbel = (gown0, gown1), (gbel0, gbel1)
    rin, din = (rin0, rin1), (din0, din1)
    relay, longs = (relay_up, relay_down), (long_up, long_down)
    n_z, n_x, n_yl, n_yh = dims["z"], dims["x"], dims["yl"], dims["yh"]
    n_core = dims["core"]
    n_row, n_col = n_yh * n_z, n_yl * n_x * n_core
    row, col = lax.axis_index("row"), lax.axis_index("col")
    yh, z = row // n_z, row % n_z
    yl, x, core = col // (n_core * n_x), (col // n_core) % n_x, col % n_core
    y_digit = yh * n_yl + yl
    n_y = n_yh * n_yl

    has_up, has_down = row > 0, row < n_row - 1
    has_left, has_right = col > 0, col < n_col - 1
    up, down = (row - 1, col), (row + 1, col)
    lft, rgt = (row, col - 1), (row, col + 1)

    turn = n_x * n_core

    def core_member(m):
        return (row, (yl * n_x + x) * n_core + m)

    def x_member(m):
        return (row, (yl * n_x + m) * n_core + core)

    def y_member(m):
        return ((m // n_yl) * n_z + z, ((m % n_yl) * n_x + x) * n_core + core)

    def z_member(m):
        return (yh * n_z + m, col)

    numbers = {}

    def number(*key):
        return numbers.setdefault(key, len(numbers))

    def load(src, dst, i):
        return pltpu.make_async_copy(src, dst, local_sem.at[i])

    loads = []
    for s in range(2):
        for c in range(2):
            loads.append(
                load(trans_hbm.at[s, :, :, pl.ds(c * N, N)], own[s].at[c], 2 * s + c)
            )
    loads.append(load(frames_hbm, frames, 4))
    loads.append(load(left_hbm, left, 5))
    loads.append(load(right_hbm, right, 6))
    for c in loads:
        c.start()

    barrier = pltpu.get_barrier_semaphore()

    def hail(dev):
        pl.semaphore_signal(barrier, inc=1, device_id=dev, device_id_type=MESH)

    for cond, dev in (
        (has_up, up),
        (has_down, down),
        (has_left, lft),
        (has_right, rgt),
    ):

        @pl.when(cond)
        def _(dev=dev):
            hail(dev)

    groups = (
        (core_member, n_core, core),
        (x_member, n_x, x),
        (y_member, n_y, y_digit),
        (z_member, n_z, z),
    )
    for member, size, me in groups:
        for k in range(1, size):
            hail(member((me + k) % size))
    hails = sum(size - 1 for _, size, _ in groups)
    for cond in (has_up, has_down, has_left, has_right):
        hails = hails + jnp.where(cond, 1, 0)
    edges = ()
    if n_yh > 1:
        edges = (
            (row, n_z + 2, (n_z - 1, col)),
            (row, n_z - 1, (n_z + 2, col)),
            (row, 1, (n_z, col)),
            (row, n_z, (1, col)),
        )
    if n_yl > 1:
        edges += (
            (col, 0, (row, turn - 1)),
            (col, turn - 1, (row, 0)),
            (col, n_col - 1, (row, turn)),
            (col, turn, (row, n_col - 1)),
        )
    for at, here, there in edges:

        @pl.when(at == here)
        def _(there=there):
            hail(there)

        hails = hails + jnp.where(at == here, 1, 0)
    pl.semaphore_wait(barrier, hails)

    def remote(src, dst, key, dev):
        i = number(*key)
        return pltpu.make_async_remote_copy(
            src_ref=src,
            dst_ref=dst,
            send_sem=send_sem.at[i],
            recv_sem=recv_sem.at[i],
            device_id=dev,
            device_id_type=MESH,
        )

    def on(cond, f):
        @pl.when(cond)
        def _():
            f()

    def both(*conds):
        return functools.reduce(jnp.logical_and, conds)

    n_pieces = len(PIECES)
    split_rows = n_yh > 1

    class Halo:
        def __init__(self, way, s):
            self.way, self.s = way, s
            self.sends, self.takes = (has_up, has_down) if way < 0 else (has_down, has_up)
            self.next = (row + way, col)
            self.edge = n_z if way < 0 else n_z - 1
            self.relay = n_row - 1 if way < 0 else 0
            self.last = self.edge + way
            self.ring = (yh * n_z + (z - way + n_z) % n_z, col)
            self.from1 = yh * n_z + (z + way + n_z) % n_z
            self.from2 = yh * n_z + (z + 2 * way + n_z) % n_z
            none = 0 if way < 0 else n_row - 1
            self.pass1 = jnp.logical_and(n_z > 2, self.from1 != none)
            self.pass2 = jnp.logical_and(n_z > 2, self.from2 != none)

        def ends(self, half, start, rows):
            here = pl.ds(start, rows)
            if self.way < 0:
                src = trans_hbm.at[self.s, :, here, pl.ds(half * N, N)]
                return src, bel[self.s].at[half, :, here]
            return gbel[self.s].at[half, :, here], din[self.s].at[half, :, here]

        def piece(self, k):
            half, start, rows, _ = PIECES[k]
            src, dst = self.ends(half, start, rows)
            return remote(src, dst, ("piece", self.way, self.s, k), self.next)

        def middle(self, k):
            first = sum(p[2] for p in PIECES[:k] if p[3])
            return relay[max(self.way, 0)].at[self.s, :, pl.ds(first, PIECES[k][2])]

        def first_leg(self, k):
            half, start, rows, _ = PIECES[k]
            src, _ = self.ends(half, start, rows)
            mid = self.middle(k)
            return remote(src, mid, ("leg", self.way, self.s, k), (self.relay, col))

        def second_leg(self, k):
            half, start, rows, _ = PIECES[k]
            _, dst = self.ends(half, start, rows)
            mid = self.middle(k)
            return remote(mid, dst, ("piece", self.way, self.s, k), (self.last, col))

        def relayed(self, k):
            return split_rows and PIECES[k][3]

        def start_piece(self, k):
            if not self.relayed(k):
                on(self.sends, self.piece(k).start)
                return
            on(both(self.sends, row != self.edge), self.piece(k).start)
            on(row == self.edge, self.first_leg(k).start)

        def pass_on(self):
            for k in range(n_pieces):
                if self.relayed(k):

                    @pl.when(row == self.relay)
                    def _(k=k):
                        self.first_leg(k).wait_recv()
                        self.second_leg(k).start()

        def wait_piece(self, k):
            on(self.takes, self.piece(k).wait_recv)

        def hop(self, h):
            src, dst = self.ends(*LONG)
            mids = longs[max(self.way, 0)]
            src = src if h == 0 else mids.at[self.s, h - 1]
            dst = dst if h == 2 else mids.at[self.s, h]
            dev = (self.from2 + self.way, col) if h == 2 else self.ring
            return remote(src, dst, ("long", self.way, self.s, h), dev)

        def start_long(self):
            on(self.sends, self.hop(0).start)

        def pass_long(self, h):
            @pl.when((self.pass1, self.pass2)[h])
            def _():
                self.hop(h).wait_recv()
                self.hop(h + 1).start()

        def wait_long(self):
            on(self.takes, self.hop(2).wait_recv)

        def finish(self):
            for k in range(n_pieces):
                if not self.relayed(k):
                    on(self.sends, self.piece(k).wait_send)
                    continue
                on(both(self.sends, row != self.edge), self.piece(k).wait_send)
                on(row == self.edge, self.first_leg(k).wait_send)
                on(row == self.relay, self.second_leg(k).wait_send)
            on(self.sends, self.hop(0).wait_send)
            on(self.pass1, self.hop(1).wait_send)
            on(self.pass2, self.hop(2).wait_send)

    fwd = Halo(-1, 0), Halo(-1, 1)
    back = Halo(1, 0), Halo(1, 1)

    class Side:
        def __init__(self, way, s):
            self.way, self.s = way, s
            self.sends, self.takes = (has_left, has_right) if way < 0 else (has_right, has_left)
            self.edge = turn if way < 0 else turn - 1
            self.relay = 0 if way < 0 else n_col - 1
            self.mid = side_mid.at[max(way, 0), s]
            if way < 0:
                self.src, self.dst = trans_hbm.at[s, :, :, pl.ds(0, N)], own[s].at[2]
            else:
                self.src, self.dst = gown[s].at[2], rin[s].at[0]
            self.relayed = n_yl > 1

        def whole(self):
            return remote(self.src, self.dst, ("side", self.way, self.s), (row, col + self.way))

        def first_leg(self):
            return remote(self.src, self.mid, ("side_leg", self.way, self.s), (row, self.relay))

        def second_leg(self):
            there = (row, self.edge + self.way)
            return remote(self.mid, self.dst, ("side", self.way, self.s), there)

        def start(self):
            if not self.relayed:
                on(self.sends, self.whole().start)
                return
            on(both(self.sends, col != self.edge), self.whole().start)
            on(col == self.edge, self.first_leg().start)

        def pass_on(self):
            if self.relayed:

                @pl.when(col == self.relay)
                def _():
                    self.first_leg().wait_recv()
                    self.second_leg().start()

        def wait(self):
            on(self.takes, self.whole().wait_recv)

        def finish(self):
            if not self.relayed:
                on(self.sends, self.whole().wait_send)
                return
            on(both(self.sends, col != self.edge), self.whole().wait_send)
            on(col == self.edge, self.first_leg().wait_send)
            on(col == self.relay, self.second_leg().wait_send)

    fwd_side = Side(-1, 0), Side(-1, 1)
    back_side = Side(1, 0), Side(1, 1)

    def fwd_corner(s):
        return remote(bel[s].at[0], bel[s].at[2], ("fwd_corner", s), lft)

    def back_corner(s):
        return remote(gbel[s].at[2], rin[s].at[1], ("back_corner", s), rgt)

    late = [k for k in range(n_pieces) if PIECES[k][0] == 0]
    early = [k for k in range(n_pieces) if PIECES[k][0] == 1]

    fwd[0].start_long()
    for k in late + early:
        fwd[0].start_piece(k)
    fwd_side[0].start()

    zero3 = jnp.zeros((2, N, N), F32)
    for s in range(2):

        @pl.when(jnp.logical_not(has_down))
        def _(s=s):
            for c in range(3):
                bel[s][c] = zero3

        @pl.when(jnp.logical_not(has_right))
        def _(s=s):
            own[s][2] = zero3
            on(has_down, functools.partial(bel[s].__setitem__, 2, zero3))

        @pl.when(jnp.logical_not(has_up))
        def _(s=s):
            for c in range(2):
                din[s][c] = zero3

        @pl.when(jnp.logical_not(has_left))
        def _(s=s):
            for c in range(2):
                rin[s][c] = zero3

    loads[4].wait()
    for c in loads[5:]:
        c.wait()

    def place(j):
        return place_ref[2 * j], place_ref[2 * j + 1]

    @pl.loop(0, batch)
    def _(j):
        counts = frames[j].astype(F32).astype(BF16)
        mixed = dot(perm_rows_ref[...], counts).astype(BF16)
        counts = dot(mixed, perm_cols_ref[...])
        base = 0.02 * jnp.exp2(lower_ref[j].astype(F32) * 0.25)
        extent = (0.1 / 255.0) * jnp.exp2(span_ref[j].astype(F32) * 0.25)

        def widen(small):
            wide = jnp.dot(
                small,
                spread_ref[...],
                precision=lax.Precision.HIGHEST,
                preferred_element_type=F32,
            )
            tall = jnp.broadcast_to(wide[:, None, :], (NBK, 8, N)).reshape(HALF, N)
            return jnp.concatenate([tall, tall], 0)

        meas[j] = widen(base) + counts * widen(extent)
        y, x = place(j)
        shift = x % N
        for p in range(2):
            wav[j, p] = pltpu.roll(pltpu.roll(probe_ref[p], shift, 1), y, 0)

    def masks(j):
        y, x = place(j)
        rows = lax.broadcasted_iota(jnp.int32, (N, N), 0) >= y
        cols = lax.broadcasted_iota(jnp.int32, (N, N), 1) >= x % N
        return rows, cols, x // N

    def take(s, j, p):
        rows, cols, k = masks(j)
        here = jnp.where(cols, own[s][k, p], own[s][k + 1, p])
        below = jnp.where(cols, bel[s][k, p], bel[s][k + 1, p])
        return jnp.where(rows, here, below)

    def arrive(s):
        for k in late:
            fwd[s].wait_piece(k)
        on(both(has_down, has_left), fwd_corner(s).start)
        fwd[s].pass_on()
        for k in early:
            fwd[s].wait_piece(k)
        fwd[s].wait_long()
        fwd_side[s].wait()
        on(both(has_down, has_right), fwd_corner(s).wait_recv)

    fwd[0].pass_long(0)
    fwd[1].start_long()
    for k in late + early:
        fwd[1].start_piece(k)
    fwd_side[1].start()
    fwd_side[0].pass_on()
    fwd[0].pass_long(1)
    fwd[1].pass_long(0)
    fwd_side[1].pass_on()
    for c in loads[:4]:
        c.wait()
    arrive(0)

    @pl.loop(0, batch)
    def _(j):
        patch = take(0, j, 0), take(0, j, 1)
        patch0[j, 0], patch0[j, 1] = patch
        wave = complex_mul((wav[j, 0], wav[j, 1]), patch)
        amp[j, 0], amp[j, 1] = transform(*wave, left, right, 0, True, True)

    fwd[1].pass_long(1)
    arrive(1)

    @pl.loop(0, batch)
    def _(j):
        patch = take(1, j, 0), take(1, j, 1)
        incoming = amp[j, 0], amp[j, 1]
        far = transform(*complex_mul(incoming, patch), left, right, 1, True, False)
        misfit = far[0] * far[0] + far[1] * far[1] - meas[j]
        wave = transform(misfit * far[0], misfit * far[1], left, right, 2, False, True)
        piece[j, 0], piece[j, 1] = conj_mul(wave, incoming)
        amp[j, 0], amp[j, 1] = conj_mul(wave, patch)

    def accumulate(s):
        @pl.loop(0, N // 8)
        def _(i):
            here = pl.ds(pl.multiple_of(i * 8, 8), 8)
            rows = lax.broadcasted_iota(jnp.int32, (8, N), 0) + i * 8
            cols = lax.broadcasted_iota(jnp.int32, (8, N), 1)
            for p in range(2):
                sums = [[jnp.zeros((8, N), F32) for _ in range(3)] for _ in range(2)]
                for j in range(batch):
                    y, x = place(j)
                    value = piece[j, p, here, :]
                    target = x // N + jnp.where(cols >= x % N, 0, 1)
                    upper = jnp.where(rows >= y, value, 0.0)
                    for r, part in enumerate((upper, value - upper)):
                        for c in range(3):
                            sums[r][c] += jnp.where(target == c, part, 0.0)
                for c in range(3):
                    gown[s][c, p, here, :] = sums[0][c]
                    gbel[s][c, p, here, :] = sums[1][c]

    def send_back(s):
        on(both(has_right, has_down), back_corner(s).start)
        back[s].start_long()
        for k in early:
            back[s].start_piece(k)
        back_side[s].start()

    def send_back_late(s):
        @pl.when(both(has_left, has_down))
        def _():
            back_corner(s).wait_recv()
            gbel[s][0] += rin[s][1]

        for k in late:
            back[s].start_piece(k)

    accumulate(1)
    send_back(1)

    gacc[...] = jnp.zeros_like(gacc)

    @pl.loop(0, batch)
    def _(j):
        on(j == batch - 3, lambda: back[1].pass_long(0))
        on(j == batch - 1, lambda: send_back_late(1))
        wave = transform(amp[j, 0], amp[j, 1], left, right, 3, True, True)
        piece[j, 0], piece[j, 1] = conj_mul(wave, (wav[j, 0], wav[j, 1]))
        term = conj_mul(wave, (patch0[j, 0], patch0[j, 1]))
        y, x = place(j)
        for p in range(2):
            turned = pltpu.roll(pltpu.roll(term[p], (N - y) % N, 0), (N - x % N) % N, 1)
            for h in range(2):
                gacc[pl.ds((2 * p + h) * N, N), :] += turned[:, h * HALF : (h + 1) * HALF]

    accumulate(0)
    back[1].pass_long(1)
    send_back(0)

    total = gacc.shape[0]
    stages = (
        (stage_core, core_member, n_core, core, "core"),
        (stage_x, x_member, n_x, x, "x"),
        (stage_y, y_member, n_y, y_digit, "y"),
        (stage_z, z_member, n_z, z, "z"),
    )
    length = total
    base = 0
    spans = []
    for stage, member, size, me, sem in stages:
        chunk = length // size
        copies = []
        for k in range(1, size):
            m = (me + k) % size
            src = gacc.at[pl.ds(pl.multiple_of(base + m * chunk, 8), chunk), :]
            copies.append(remote(src, stage.at[k - 1], ("sum", sem, k), member(m)))
        for c in copies:
            c.start()
        spans.append((base, length, chunk))
        base = base + me * chunk
        mine = pl.ds(pl.multiple_of(base, 8), chunk)
        for c in copies:
            c.wait()
        got = gacc[mine, :]
        for k in range(1, size):
            got = got + stage[k - 1]
        gacc[mine, :] = got
        length = chunk
        if sem == "core":
            back[1].pass_on()
            back_side[1].pass_on()
        if sem == "x":
            send_back_late(0)
        if sem == "y":
            back[0].pass_long(0)
        if sem == "z":
            back[0].pass_on()
            back_side[0].pass_on()

    mine = pl.ds(pl.multiple_of(base, 8), length)
    newprobe_ref[mine, :] = gacc[mine, :]
    for (stage, member, size, me, sem), (start, length, chunk) in reversed(
        list(zip(stages, spans))
    ):
        held = newprobe_ref.at[pl.ds(pl.multiple_of(start + me * chunk, 8), chunk), :]
        copies = [
            remote(held, held, ("whole", sem, k), member((me + k) % size))
            for k in range(1, size)
        ]
        for c in copies:
            c.start()
        for k, c in enumerate(copies, 1):
            c.wait_send()
            m = (me - k + size) % size
            there = newprobe_ref.at[pl.ds(pl.multiple_of(start + m * chunk, 8), chunk), :]
            remote(there, there, ("whole", sem, k), member(m)).wait_recv()
        if sem == "y":
            back[0].pass_long(1)

    for s in (1, 0):
        back_side[s].wait()
        for k in range(n_pieces):
            back[s].wait_piece(k)
        back[s].wait_long()
        for c in range(2):
            for p in range(2):
                value = gown[s][c, p] + din[s][c, p]
                if c == 0:
                    value = value + rin[s][0, p]
                grad_ref[s, p, :, pl.ds(c * N, N)] = value

    for s in range(2):
        fwd[s].finish()
        back[s].finish()
        fwd_side[s].finish()
        on(both(has_down, has_left), fwd_corner(s).wait_send)
        on(both(has_right, has_down), back_corner(s).wait_send)
        back_side[s].finish()
    assert len(numbers) <= N_SEMS


def body(dims, transmission, probe, offsets, frames, lower_level, level_span):
    batch = offsets.shape[0]
    layers, _, rows, cols = transmission.shape
    anchor = jnp.stack([lax.axis_index("row") * rows, lax.axis_index("col") * cols])
    place = (offsets - anchor[None, :]).reshape(2 * batch)
    left, right = tables()
    perm_rows, perm_cols, spread = permutation()
    n_y = dims["yh"] * dims["yl"]
    total = 2 * 2 * N
    chunk_core = total // dims["core"]
    chunk_x = chunk_core // dims["x"]
    chunk_y = chunk_x // n_y
    chunk_z = chunk_y // dims["z"]
    count_all = batch * lax.axis_size("row") * lax.axis_size("col")
    rate = PROBE_RATE / math.sqrt(count_all)
    any_space = pl.BlockSpec(memory_space=pl.ANY)
    vmem = pl.BlockSpec(memory_space=pltpu.VMEM)
    smem = pl.BlockSpec(memory_space=pltpu.SMEM)

    def block(*shape, dtype=F32):
        return pltpu.VMEM(shape, dtype)

    tile = [block(3, 2, N, N) for _ in range(8)]
    arriving = [block(2, 2, N, N) for _ in range(4)]
    scratch = (
        tile
        + arriving
        + [block(2, 2, sum(p[2] for p in PIECES if p[3]), N) for _ in range(2)]
        + [block(2, 2, 2, LONG[2], N) for _ in range(2)]
        + [block(2, 2, 2, N, N)]
        + [
            block(batch, N, N, dtype=jnp.int32),
            block(8, N, 3 * N, dtype=BF16),
            block(8, 3 * N, N, dtype=BF16),
            block(batch, N, N),
            block(batch, 2, N, N),
            block(batch, 2, N, N),
            block(batch, 2, N, N),
            block(batch, 2, N, N),
            block(total, HALF),
            block(1, chunk_core, HALF),
            block(max(dims["x"] - 1, 1), chunk_x, HALF),
            block(max(n_y - 1, 1), chunk_y, HALF),
            block(max(dims["z"] - 1, 1), chunk_z, HALF),
            pltpu.SemaphoreType.DMA((7,)),
            pltpu.SemaphoreType.DMA((N_SEMS,)),
            pltpu.SemaphoreType.DMA((N_SEMS,)),
        ]
    )
    gradient, probe_sum = pl.pallas_call(
        functools.partial(kernel, batch, rate, dims),
        out_shape=(
            jax.ShapeDtypeStruct(transmission.shape, F32),
            jax.ShapeDtypeStruct((total, HALF), F32),
        ),
        in_specs=[smem, any_space, vmem, any_space, vmem, vmem, any_space, any_space]
        + [vmem] * 3,
        out_specs=(vmem, vmem),
        scratch_shapes=scratch,
        compiler_params=pltpu.CompilerParams(
            collective_id=0, has_side_effects=True, vmem_limit_bytes=62 * 2**20
        ),
        name="ptycho_step",
    )(
        place,
        transmission,
        probe,
        frames,
        lower_level,
        level_span,
        left,
        right,
        perm_rows,
        perm_cols,
        spread,
    )
    summed = probe_sum.reshape(2, 2, N, HALF).transpose(0, 2, 1, 3).reshape(2, N, N)
    return transmission - OBJECT_RATE * gradient, probe - rate * summed


def solution(mesh):
    in_specs = (
        P(None, None, "row", "col"),
        P(),
        P(("row", "col"), None),
        P(("row", "col"), None, None),
        P(("row", "col"), None, None),
        P(("row", "col"), None, None),
    )
    out_specs = (P(None, None, "row", "col"), P())
    return jax.shard_map(
        functools.partial(body, DIMS),
        mesh=mesh,
        in_specs=in_specs,
        out_specs=out_specs,
        check_vma=False,
    )
```

```python
import functools
import math

import jax
import jax.numpy as jnp
import numpy as np
from jax import lax
from jax.experimental import pallas as pl
from jax.experimental.pallas import tpu as pltpu
from jax.sharding import PartitionSpec as P

PROPAGATION = 0.5
OBJECT_RATE = 0.1
PROBE_RATE = 0.5
N = 256
HALF = 128
NBK = 16
DIMS = dict(yh=2, z=4, yl=2, x=4, core=2)
MESH = pl.DeviceIdType.MESH
PIECES = ((0, 0, 256, False), (1, 0, 168, True))
LONG = (1, 168, 88)
N_SEMS = 96
GROUP = 2
F32 = jnp.float32
BF16 = jnp.bfloat16


def block_pairs():
    n = np.arange(N)
    dft = np.exp(-2j * np.pi * np.outer(n, n) / N) / math.sqrt(N)
    freq = np.where(n < HALF, n, n - N).astype(np.float64)
    chirp = np.exp(-1j * np.pi * PROPAGATION * freq * freq / N)
    prop = dft.conj().T @ (chirp[:, None] * dft)
    fu, fv = dft[0::2, :HALF], dft[1::2, :HALF]
    first, second = prop[:HALF, :HALF], prop[:HALF, HALF:]
    cu, cv = (first + second) / 2, (first - second) / 2
    return {
        "prop": (cu, cv),
        "dft": (fu, fv),
        "idft": (fu.conj().T, fv.conj().T),
        "adj": (cu.conj().T, cv.conj().T),
    }


ORDER = ("prop", "dft", "idft", "adj")


def tables():
    left, right = [], []
    pairs = block_pairs()
    for name in ORDER:
        for m in pairs[name]:
            real = np.block([[m.real, -m.imag], [m.imag, m.real]]).astype(np.float32)
            hi = np.asarray(real, dtype=jnp.bfloat16)
            lo = np.asarray(real - hi.astype(np.float32), dtype=jnp.bfloat16)
            left.append(np.concatenate([hi, hi, lo], 1))
            right.append(np.concatenate([hi.T, hi.T, lo.T], 0))
    return np.stack(left), np.stack(right)


def permutation():
    perm = np.zeros((N, N), np.float32)
    for p in range(N):
        perm[p, 2 * p if p < HALF else 2 * (p - HALF) + 1] = 1
    rows = np.asarray(perm, dtype=jnp.bfloat16)
    cols = np.asarray(perm.T, dtype=jnp.bfloat16)
    spread = np.zeros((NBK, N), np.float32)
    for p in range(N):
        spread[(p % HALF) // 8, p] = 1
    return rows, cols, spread


def split(x):
    hi = x.astype(BF16)
    lo = (x - hi.astype(F32)).astype(BF16)
    return hi, lo


def dot(a, b):
    return jnp.dot(a, b, preferred_element_type=F32)


def along_cols(re, im, right_ref, op, pre, post):
    a, b, c, d = re[:, :HALF], re[:, HALF:], im[:, :HALF], im[:, HALF:]
    if pre:
        u = jnp.concatenate([a + b, c + d], 1)
        v = jnp.concatenate([a - b, c - d], 1)
    else:
        u = jnp.concatenate([a, c], 1)
        v = jnp.concatenate([b, d], 1)
    out = []
    for i, x in enumerate((u, v)):
        hi, lo = split(x)
        out.append(dot(jnp.concatenate([hi, lo, hi], 1), right_ref[2 * op + i]))
    yu, yv = out
    if post:
        p, m = yu + yv, yu - yv
    else:
        p, m = yu, yv
    return (
        jnp.concatenate([p[:, :HALF], m[:, :HALF]], 1),
        jnp.concatenate([p[:, HALF:], m[:, HALF:]], 1),
    )


def along_rows(re, im, left_ref, op, pre, post):
    a, b, c, d = re[:HALF], re[HALF:], im[:HALF], im[HALF:]
    if pre:
        u = jnp.concatenate([a + b, c + d], 0)
        v = jnp.concatenate([a - b, c - d], 0)
    else:
        u = jnp.concatenate([a, c], 0)
        v = jnp.concatenate([b, d], 0)
    out = []
    for i, x in enumerate((u, v)):
        hi, lo = split(x)
        out.append(dot(left_ref[2 * op + i], jnp.concatenate([hi, lo, hi], 0)))
    yu, yv = out
    if post:
        p, m = yu + yv, yu - yv
    else:
        p, m = yu, yv
    return (
        jnp.concatenate([p[:HALF], m[:HALF]], 0),
        jnp.concatenate([p[HALF:], m[HALF:]], 0),
    )


def transform(re, im, left_ref, right_ref, op, pre, post):
    re, im = along_cols(re, im, right_ref, op, pre, post)
    return along_rows(re, im, left_ref, op, pre, post)


def transforms(waves, left_ref, right_ref, op, pre, post):
    waves = [along_cols(*w, right_ref, op, pre, post) for w in waves]
    return [along_rows(*w, left_ref, op, pre, post) for w in waves]


def complex_mul(a, b):
    return a[0] * b[0] - a[1] * b[1], a[0] * b[1] + a[1] * b[0]


def conj_mul(a, b):
    return a[0] * b[0] + a[1] * b[1], a[1] * b[0] - a[0] * b[1]


def kernel(
    batch,
    rate,
    dims,
    offset_hbm,
    trans_hbm,
    probe_hbm,
    frames_hbm,
    lower_hbm,
    span_hbm,
    left_hbm,
    right_hbm,
    perm_rows_hbm,
    perm_cols_hbm,
    spread_hbm,
    newtrans_hbm,
    newprobe_hbm,
    own0,
    own1,
    bel0,
    bel1,
    gown0,
    gown1,
    gbel0,
    gbel1,
    rin0,
    rin1,
    din0,
    din1,
    relay_up,
    relay_down,
    long_up,
    long_down,
    side_mid,
    offset_ref,
    frames,
    left,
    right,
    probe_ref,
    lower_ref,
    span_ref,
    perm_rows_ref,
    perm_cols_ref,
    spread_ref,
    meas,
    wav,
    patch0,
    amp,
    piece,
    gacc,
    gfull,
    stage_core,
    stage_plane,
    stage_z,
    local_sem,
    send_sem,
    recv_sem,
):
    own, bel = (own0, own1), (bel0, bel1)
    gown, gbel = (gown0, gown1), (gbel0, gbel1)
    rin, din = (rin0, rin1), (din0, din1)
    relay, longs = (relay_up, relay_down), (long_up, long_down)
    n_z, n_x, n_yl, n_yh = dims["z"], dims["x"], dims["yl"], dims["yh"]
    n_core = dims["core"]
    n_row, n_col = n_yh * n_z, n_yl * n_x * n_core
    row, col = lax.axis_index("row"), lax.axis_index("col")
    yh, z = row // n_z, row % n_z
    yl, x, core = col // (n_core * n_x), (col // n_core) % n_x, col % n_core
    y_digit = yh * n_yl + yl
    n_y = n_yh * n_yl

    has_up, has_down = row > 0, row < n_row - 1
    has_left, has_right = col > 0, col < n_col - 1
    up, down = (row - 1, col), (row + 1, col)
    lft, rgt = (row, col - 1), (row, col + 1)

    turn = n_x * n_core

    def core_member(m):
        return (row, (yl * n_x + x) * n_core + m)

    def plane_member(m):
        y, x = m // n_x, m % n_x
        return ((y // n_yl) * n_z + z, ((y % n_yl) * n_x + x) * n_core + core)

    def z_member(m):
        return (yh * n_z + m, col)

    numbers = {}

    def number(*key):
        return numbers.setdefault(key, len(numbers))

    def load(src, dst, i):
        return pltpu.make_async_copy(src, dst, local_sem.at[i])

    loads = []
    for s in range(2):
        for c in range(2):
            loads.append(
                load(trans_hbm.at[s, :, :, pl.ds(c * N, N)], own[s].at[c], 2 * s + c)
            )
    for src, dst in (
        (offset_hbm, offset_ref),
        (frames_hbm, frames),
        (probe_hbm, probe_ref),
        (lower_hbm, lower_ref),
        (span_hbm, span_ref),
        (perm_rows_hbm, perm_rows_ref),
        (perm_cols_hbm, perm_cols_ref),
        (spread_hbm, spread_ref),
        (left_hbm, left),
        (right_hbm, right),
    ):
        loads.append(load(src, dst, len(loads)))

    barrier = pltpu.get_barrier_semaphore()

    def hail(dev):
        pl.semaphore_signal(barrier, inc=1, device_id=dev, device_id_type=MESH)

    for cond, dev in (
        (has_up, up),
        (has_down, down),
        (has_left, lft),
        (has_right, rgt),
    ):

        @pl.when(cond)
        def _(dev=dev):
            hail(dev)

    groups = (
        (core_member, n_core, core),
        (plane_member, n_y * n_x, y_digit * n_x + x),
        (z_member, n_z, z),
    )
    for member, size, me in groups:
        for k in range(1, size):
            hail(member((me + k) % size))
    hails = sum(size - 1 for _, size, _ in groups)
    for cond in (has_up, has_down, has_left, has_right):
        hails = hails + jnp.where(cond, 1, 0)
    edges = ()
    if n_yh > 1:
        edges = (
            (row, n_z + 2, (n_z - 1, col)),
            (row, n_z - 1, (n_z + 2, col)),
            (row, 1, (n_z, col)),
            (row, n_z, (1, col)),
        )
    if n_yl > 1:
        edges += (
            (col, 0, (row, turn - 1)),
            (col, turn - 1, (row, 0)),
            (col, n_col - 1, (row, turn)),
            (col, turn, (row, n_col - 1)),
        )
    for at, here, there in edges:

        @pl.when(at == here)
        def _(there=there):
            hail(there)

        hails = hails + jnp.where(at == here, 1, 0)
    pl.semaphore_wait(barrier, hails)

    def remote(src, dst, key, dev):
        i = number(*key)
        return pltpu.make_async_remote_copy(
            src_ref=src,
            dst_ref=dst,
            send_sem=send_sem.at[i],
            recv_sem=recv_sem.at[i],
            device_id=dev,
            device_id_type=MESH,
        )

    def on(cond, f):
        @pl.when(cond)
        def _():
            f()

    def both(*conds):
        return functools.reduce(jnp.logical_and, conds)

    n_pieces = len(PIECES)
    split_rows = n_yh > 1

    class Halo:
        def __init__(self, way, s):
            self.way, self.s = way, s
            self.sends, self.takes = (has_up, has_down) if way < 0 else (has_down, has_up)
            self.next = (row + way, col)
            self.edge = n_z if way < 0 else n_z - 1
            self.relay = n_row - 1 if way < 0 else 0
            self.last = self.edge + way
            self.ring = (yh * n_z + (z - way + n_z) % n_z, col)
            self.from1 = yh * n_z + (z + way + n_z) % n_z
            self.from2 = yh * n_z + (z + 2 * way + n_z) % n_z
            none = 0 if way < 0 else n_row - 1
            self.pass1 = jnp.logical_and(n_z > 2, self.from1 != none)
            self.pass2 = jnp.logical_and(n_z > 2, self.from2 != none)

        def ends(self, half, start, rows):
            here = pl.ds(start, rows)
            if self.way < 0:
                src = trans_hbm.at[self.s, :, here, pl.ds(half * N, N)]
                return src, bel[self.s].at[half, :, here]
            return gbel[self.s].at[half, :, here], din[self.s].at[half, :, here]

        def piece(self, k):
            half, start, rows, _ = PIECES[k]
            src, dst = self.ends(half, start, rows)
            return remote(src, dst, ("piece", self.way, self.s, k), self.next)

        def middle(self, k):
            first = sum(p[2] for p in PIECES[:k] if p[3])
            return relay[max(self.way, 0)].at[self.s, :, pl.ds(first, PIECES[k][2])]

        def first_leg(self, k):
            half, start, rows, _ = PIECES[k]
            src, _ = self.ends(half, start, rows)
            mid = self.middle(k)
            return remote(src, mid, ("leg", self.way, self.s, k), (self.relay, col))

        def second_leg(self, k):
            half, start, rows, _ = PIECES[k]
            _, dst = self.ends(half, start, rows)
            mid = self.middle(k)
            return remote(mid, dst, ("piece", self.way, self.s, k), (self.last, col))

        def relayed(self, k):
            return split_rows and PIECES[k][3]

        def start_piece(self, k):
            if not self.relayed(k):
                on(self.sends, self.piece(k).start)
            else:
                on(both(self.sends, row != self.edge), self.piece(k).start)

        def start_legs(self):
            for k in range(n_pieces):
                if self.relayed(k):
                    on(row == self.edge, self.first_leg(k).start)

        def pass_on(self):
            for k in range(n_pieces):
                if self.relayed(k):

                    @pl.when(row == self.relay)
                    def _(k=k):
                        self.first_leg(k).wait_recv()
                        self.second_leg(k).start()

        def wait_piece(self, k):
            on(self.takes, self.piece(k).wait_recv)

        def hop(self, h):
            src, dst = self.ends(*LONG)
            mids = longs[max(self.way, 0)]
            src = src if h == 0 else mids.at[self.s, h - 1]
            dst = dst if h == 2 else mids.at[self.s, h]
            dev = (self.from2 + self.way, col) if h == 2 else self.ring
            return remote(src, dst, ("long", self.way, self.s, h), dev)

        def start_long(self):
            on(self.sends, self.hop(0).start)

        def pass_long(self, h):
            @pl.when((self.pass1, self.pass2)[h])
            def _():
                self.hop(h).wait_recv()
                self.hop(h + 1).start()

        def wait_long(self):
            on(self.takes, self.hop(2).wait_recv)

        def finish(self):
            for k in range(n_pieces):
                if not self.relayed(k):
                    on(self.sends, self.piece(k).wait_send)
                    continue
                on(both(self.sends, row != self.edge), self.piece(k).wait_send)
                on(row == self.edge, self.first_leg(k).wait_send)
                on(row == self.relay, self.second_leg(k).wait_send)
            on(self.sends, self.hop(0).wait_send)
            on(self.pass1, self.hop(1).wait_send)
            on(self.pass2, self.hop(2).wait_send)

    fwd = Halo(-1, 0), Halo(-1, 1)
    back = Halo(1, 0), Halo(1, 1)

    class Side:
        def __init__(self, way, s):
            self.way, self.s = way, s
            self.sends, self.takes = (has_left, has_right) if way < 0 else (has_right, has_left)
            self.edge = turn if way < 0 else turn - 1
            self.relay = 0 if way < 0 else n_col - 1
            self.mid = side_mid.at[max(way, 0), s]
            if way < 0:
                self.src, self.dst = trans_hbm.at[s, :, :, pl.ds(0, N)], own[s].at[2]
            else:
                self.src, self.dst = gown[s].at[2], rin[s].at[0]
            self.relayed = n_yl > 1

        def whole(self):
            return remote(self.src, self.dst, ("side", self.way, self.s), (row, col + self.way))

        def first_leg(self):
            return remote(self.src, self.mid, ("side_leg", self.way, self.s), (row, self.relay))

        def second_leg(self):
            there = (row, self.edge + self.way)
            return remote(self.mid, self.dst, ("side", self.way, self.s), there)

        def start(self):
            if not self.relayed:
                on(self.sends, self.whole().start)
            else:
                on(both(self.sends, col != self.edge), self.whole().start)

        def start_leg(self):
            if self.relayed:
                on(col == self.edge, self.first_leg().start)

        def pass_on(self):
            if self.relayed:

                @pl.when(col == self.relay)
                def _():
                    self.first_leg().wait_recv()
                    self.second_leg().start()

        def wait(self):
            on(self.takes, self.whole().wait_recv)

        def finish(self):
            if not self.relayed:
                on(self.sends, self.whole().wait_send)
                return
            on(both(self.sends, col != self.edge), self.whole().wait_send)
            on(col == self.edge, self.first_leg().wait_send)
            on(col == self.relay, self.second_leg().wait_send)

    fwd_side = Side(-1, 0), Side(-1, 1)
    back_side = Side(1, 0), Side(1, 1)

    def fwd_corner(s):
        return remote(bel[s].at[0], bel[s].at[2], ("fwd_corner", s), lft)

    def back_corner(s):
        return remote(gbel[s].at[2], rin[s].at[1], ("back_corner", s), rgt)

    late = [k for k in range(n_pieces) if PIECES[k][0] == 0]
    early = [k for k in range(n_pieces) if PIECES[k][0] == 1]

    fwd[0].start_long()
    fwd[0].start_legs()
    for k in late + early:
        fwd[0].start_piece(k)
    fwd_side[0].start_leg()
    fwd_side[0].start()

    for c in loads:
        c.start()

    zero3 = jnp.zeros((2, N, N), F32)
    for s in range(2):

        @pl.when(jnp.logical_not(has_down))
        def _(s=s):
            for c in range(3):
                bel[s][c] = zero3

        @pl.when(jnp.logical_not(has_right))
        def _(s=s):
            own[s][2] = zero3
            on(has_down, functools.partial(bel[s].__setitem__, 2, zero3))

        @pl.when(jnp.logical_not(has_up))
        def _(s=s):
            for c in range(2):
                din[s][c] = zero3

        @pl.when(jnp.logical_not(has_left))
        def _(s=s):
            for c in range(2):
                rin[s][c] = zero3

    for c in loads[4:]:
        c.wait()

    def place(j):
        return offset_ref[0, j] & (N - 1), offset_ref[1, j] & (2 * N - 1)

    @pl.loop(0, batch)
    def _(j):
        counts = frames[j].astype(F32).astype(BF16)
        mixed = dot(perm_rows_ref[...], counts).astype(BF16)
        counts = dot(mixed, perm_cols_ref[...])
        base = 0.02 * jnp.exp2(lower_ref[j].astype(F32) * 0.25)
        extent = (0.1 / 255.0) * jnp.exp2(span_ref[j].astype(F32) * 0.25)

        def widen(small):
            wide = jnp.dot(
                small,
                spread_ref[...],
                precision=lax.Precision.HIGHEST,
                preferred_element_type=F32,
            )
            tall = jnp.broadcast_to(wide[:, None, :], (NBK, 8, N)).reshape(HALF, N)
            return jnp.concatenate([tall, tall], 0)

        meas[j] = widen(base) + counts * widen(extent)
        y, x = place(j)
        shift = x % N
        for p in range(2):
            wav[j, p] = pltpu.roll(pltpu.roll(probe_ref[p], shift, 1), y, 0)

    def masks(j):
        y, x = place(j)
        rows = lax.broadcasted_iota(jnp.int32, (N, N), 0) >= y
        cols = lax.broadcasted_iota(jnp.int32, (N, N), 1) >= x % N
        return rows, cols, x // N

    def take(s, j, p):
        rows, cols, k = masks(j)
        here = jnp.where(cols, own[s][k, p], own[s][k + 1, p])
        below = jnp.where(cols, bel[s][k, p], bel[s][k + 1, p])
        return jnp.where(rows, here, below)

    def arrive(s):
        for k in late:
            fwd[s].wait_piece(k)
        on(both(has_down, has_left), fwd_corner(s).start)
        fwd[s].pass_on()
        for k in early:
            fwd[s].wait_piece(k)
        fwd[s].wait_long()
        fwd_side[s].wait()
        on(both(has_down, has_right), fwd_corner(s).wait_recv)

    fwd[0].pass_long(0)
    fwd[1].start_long()
    fwd[1].start_legs()
    for k in late + early:
        fwd[1].start_piece(k)
    fwd_side[1].start_leg()
    fwd_side[1].start()
    fwd_side[0].pass_on()
    fwd[0].pass_long(1)
    fwd[1].pass_long(0)
    fwd_side[1].pass_on()
    for c in loads[:4]:
        c.wait()
    arrive(0)

    @pl.loop(0, batch)
    def _(j):
        patch = take(0, j, 0), take(0, j, 1)
        patch0[j, 0], patch0[j, 1] = patch
        wave = complex_mul((wav[j, 0], wav[j, 1]), patch)
        amp[j, 0], amp[j, 1] = transform(*wave, left, right, 0, True, True)

    fwd[1].pass_long(1)
    arrive(1)

    @pl.loop(0, batch // GROUP)
    def _(i):
        js = [GROUP * i + k for k in range(GROUP)]
        patches = [(take(1, j, 0), take(1, j, 1)) for j in js]
        incoming = [(amp[j, 0], amp[j, 1]) for j in js]
        far = [complex_mul(a, t) for a, t in zip(incoming, patches)]
        far = transforms(far, left, right, 1, True, False)
        misfit = [re * re + im * im - meas[j] for (re, im), j in zip(far, js)]
        waves = [(m * re, m * im) for m, (re, im) in zip(misfit, far)]
        waves = transforms(waves, left, right, 2, False, True)
        for j, wave, a, t in zip(js, waves, incoming, patches):
            piece[j, 0], piece[j, 1] = conj_mul(wave, a)
            amp[j, 0], amp[j, 1] = conj_mul(wave, t)

    def accumulate(s, below):
        total = gbel[s] if below else gown[s]

        @pl.loop(0, N // 8)
        def _(i):
            here = pl.ds(pl.multiple_of(i * 8, 8), 8)
            rows = lax.broadcasted_iota(jnp.int32, (8, N), 0) + i * 8
            cols = lax.broadcasted_iota(jnp.int32, (8, N), 1)
            sums = [[jnp.zeros((8, N), F32) for _ in range(3)] for _ in range(2)]
            for j in range(batch):
                y, x = place(j)
                inside = rows < y if below else rows >= y
                target = x // N + jnp.where(cols >= x % N, 0, 1)
                target = jnp.where(inside, target, 3)
                for c in range(3):
                    there = target == c
                    for p in range(2):
                        sums[p][c] += jnp.where(there, piece[j, p, here, :], 0.0)
            for p in range(2):
                for c in range(3):
                    total[c, p, here, :] = sums[p][c]

    def send_back_late(s):
        @pl.when(both(has_left, has_down))
        def _():
            back_corner(s).wait_recv()
            gbel[s][0] += rin[s][1]

        for k in late:
            back[s].start_piece(k)

    accumulate(1, True)
    on(both(has_right, has_down), back_corner(1).start)
    back[1].start_long()
    back[1].start_legs()
    for k in early:
        back[1].start_piece(k)
    accumulate(1, False)
    back_side[1].start_leg()
    back_side[1].start()

    gacc[...] = jnp.zeros_like(gacc)

    @pl.loop(0, batch // GROUP)
    def _(i):
        on(i == batch // GROUP - 1, lambda: back[1].pass_long(0))
        js = [GROUP * i + k for k in range(GROUP)]
        waves = [(amp[j, 0], amp[j, 1]) for j in js]
        first = [(wav[j, 0], wav[j, 1]) for j in js]
        patches = [(patch0[j, 0], patch0[j, 1]) for j in js]
        waves = transforms(waves, left, right, 3, True, True)
        terms = [conj_mul(w, t) for w, t in zip(waves, patches)]
        grads = [conj_mul(w, a) for w, a in zip(waves, first)]
        for p in range(2):
            turned = 0.0
            for j, term in zip(js, terms):
                y, x = place(j)
                turned += pltpu.roll(pltpu.roll(term[p], (N - y) % N, 0), (N - x % N) % N, 1)
            for h in range(2):
                gacc[pl.ds((2 * p + h) * N, N), :] += turned[:, h * HALF : (h + 1) * HALF]
        for j, grad in zip(js, grads):
            piece[j, 0], piece[j, 1] = grad

    send_back_late(1)

    chunks = [gacc.shape[0]]
    for _, size, _ in groups[:2]:
        chunks.append(chunks[-1] // size)
    starts = [0]
    for chunk, (_, _, me) in zip(chunks[1:], groups):
        starts.append(starts[-1] + me * chunk)
    stages = stage_core, stage_plane

    def part(ref, start, chunk):
        return ref.at[pl.ds(pl.multiple_of(start, 8), chunk), :]

    def scatter_start(g):
        member, size, me = groups[g]
        copies = []
        for k in range(1, size):
            m = (me + k) % size
            src = part(gacc, starts[g] + m * chunks[g + 1], chunks[g + 1])
            copies.append(remote(src, stages[g].at[k - 1], ("sum", g, k), member(m)))
        for c in copies:
            c.start()
        return copies

    def scatter_finish(g, copies):
        for c in copies:
            c.wait()
        mine = part(gacc, starts[g + 1], chunks[g + 1])
        got = mine[...]
        for k in range(1, groups[g][1]):
            got = got + stages[g][k - 1]
        mine[...] = got

    def gather_start(g):
        member, size, me = groups[g]
        held = part(gfull, starts[g + 1], chunks[g + 1])
        copies = [
            remote(held, held, ("whole", g, k), member((me + k) % size))
            for k in range(1, size)
        ]
        for c in copies:
            c.start()
        return copies

    def gather_finish(g, copies):
        member, size, me = groups[g]
        for k, c in enumerate(copies, 1):
            c.wait_send()
            m = (me - k + size) % size
            there = part(gfull, starts[g] + m * chunks[g + 1], chunks[g + 1])
            remote(there, there, ("whole", g, k), member(m)).wait_recv()

    stores = []

    def finish_tile(s):
        for c in (1, 0):
            for k in late if c == 0 else early:
                back[s].wait_piece(k)
            if c == 0:
                back_side[s].wait()
            else:
                back[s].wait_long()
            for p in range(2):
                value = gown[s][c, p] + din[s][c, p]
                if c == 0:
                    value = value + rin[s][0, p]
                own[s][c, p] = own[s][c, p] - OBJECT_RATE * value
            dst = newtrans_hbm.at[s, :, :, pl.ds(c * N, N)]
            stores.append(load(own[s].at[c], dst, len(stores)))
            stores[-1].start()

    copies = scatter_start(0)
    accumulate(0, True)
    for k in early:
        back[0].start_piece(k)
    back[0].start_legs()
    scatter_finish(0, copies)
    copies = scatter_start(1)
    on(both(has_right, has_down), back_corner(0).start)
    back[1].pass_long(1)
    back[0].start_long()
    back[1].pass_on()
    accumulate(0, False)
    back_side[0].start_leg()
    back_side[0].start()
    scatter_finish(1, copies)

    mine = part(gacc, starts[2], chunks[2])
    copies = [
        remote(mine, stage_z.at[z], ("sum", 3, k), z_member((z + k) % n_z))
        for k in range(1, n_z)
    ]
    for c in copies:
        c.start()
    stage_z[z] = mine[...]
    back_side[1].pass_on()
    send_back_late(0)
    back[0].pass_long(0)
    back[0].pass_on()
    for c in copies:
        c.wait()
    got = stage_z[0]
    for m in range(1, n_z):
        got = got + stage_z[m]
    part(gfull, starts[2], chunks[2])[...] = got

    copies = gather_start(1)
    back_side[0].pass_on()
    back[0].pass_long(1)
    gather_finish(1, copies)
    copies = gather_start(0)
    finish_tile(1)
    gather_finish(0, copies)

    for p in range(2):
        for h in range(2):
            cols = pl.ds(h * HALF, HALF)
            summed = gfull[pl.ds((2 * p + h) * N, N), :]
            probe_ref[p, :, cols] = probe_ref[p, :, cols] - rate * summed
    stores.append(load(probe_ref, newprobe_hbm, len(stores)))
    stores[-1].start()

    finish_tile(0)
    for c in stores:
        c.wait()

    for s in range(2):
        fwd[s].finish()
        back[s].finish()
        fwd_side[s].finish()
        on(both(has_down, has_left), fwd_corner(s).wait_send)
        on(both(has_right, has_down), back_corner(s).wait_send)
        back_side[s].finish()
    assert len(numbers) <= N_SEMS


def hand_on(trans, probe, out_trans, out_probe, held, held_probe, sems):
    pieces = [(probe.at[p], held_probe.at[p], out_probe.at[p]) for p in range(2)]
    for s in range(2):
        for p in range(2):
            for k in range(2):
                at = s, p, pl.ds(k * HALF, HALF)
                pieces.append((trans.at[at], held.at[at], out_trans.at[at]))
    takes, gives = [], []
    for i, (src, mid, dst) in enumerate(pieces):
        takes.append(pltpu.make_async_copy(src, mid, sems.at[0, i]))
        gives.append(pltpu.make_async_copy(mid, dst, sems.at[1, i]))
    for take in takes:
        take.start()
    for take, give in zip(takes, gives):
        take.wait()
        give.start()
    for give in gives:
        give.wait()


def body(dims, transmission, probe, offsets, frames, lower_level, level_span):
    batch = offsets.shape[0]
    left, right = tables()
    perm_rows, perm_cols, spread = permutation()
    n_y = dims["yh"] * dims["yl"]
    total = 2 * 2 * N
    chunk_core = total // dims["core"]
    members = n_y * dims["x"]
    chunk_plane = chunk_core // members
    count_all = batch * lax.axis_size("row") * lax.axis_size("col")
    rate = PROBE_RATE / math.sqrt(count_all)
    any_space = pl.BlockSpec(memory_space=pl.ANY)

    def block(*shape, dtype=F32):
        return pltpu.VMEM(shape, dtype)

    tile = [block(3, 2, N, N) for _ in range(8)]
    arriving = [block(2, 2, N, N) for _ in range(4)]
    scratch = (
        tile
        + arriving
        + [block(2, 2, sum(p[2] for p in PIECES if p[3]), N) for _ in range(2)]
        + [block(2, 2, 2, LONG[2], N) for _ in range(2)]
        + [block(2, 2, 2, N, N)]
        + [
            pltpu.SMEM((2, batch), jnp.int32),
            block(batch, N, N, dtype=jnp.int32),
            block(8, N, 3 * N, dtype=BF16),
            block(8, 3 * N, N, dtype=BF16),
            block(2, N, N),
            block(batch, NBK, NBK, dtype=jnp.int32),
            block(batch, NBK, NBK, dtype=jnp.int32),
            block(N, N, dtype=BF16),
            block(N, N, dtype=BF16),
            block(NBK, N),
            block(batch, N, N),
            block(batch, 2, N, N),
            block(batch, 2, N, N),
            block(batch, 2, N, N),
            block(batch, 2, N, N),
            block(total, HALF),
            block(total, HALF),
            block(1, chunk_core, HALF),
            block(max(members - 1, 1), chunk_plane, HALF),
            block(dims["z"], chunk_plane, HALF),
            pltpu.SemaphoreType.DMA((14,)),
            pltpu.SemaphoreType.DMA((N_SEMS,)),
            pltpu.SemaphoreType.DMA((N_SEMS,)),
        ]
    )
    results = pl.pallas_call(
        functools.partial(kernel, batch, rate, dims),
        out_shape=(
            jax.ShapeDtypeStruct(transmission.shape, F32),
            jax.ShapeDtypeStruct(probe.shape, F32),
        ),
        in_specs=[any_space] * 11,
        out_specs=(any_space, any_space),
        scratch_shapes=scratch,
        compiler_params=pltpu.CompilerParams(
            collective_id=0, has_side_effects=True, vmem_limit_bytes=62 * 2**20
        ),
        name="ptycho_step",
    )(
        offsets.T,
        transmission,
        probe,
        frames,
        lower_level,
        level_span,
        left,
        right,
        perm_rows,
        perm_cols,
        spread,
    )
    return pl.pallas_call(
        hand_on,
        out_shape=tuple(jax.ShapeDtypeStruct(r.shape, r.dtype) for r in results),
        in_specs=[any_space] * 2,
        out_specs=(any_space, any_space),
        scratch_shapes=[
            block(*transmission.shape),
            block(*probe.shape),
            pltpu.SemaphoreType.DMA((2, 10)),
        ],
        name="hand_on",
    )(*results)


def solution(mesh):
    in_specs = (
        P(None, None, "row", "col"),
        P(),
        P(("row", "col"), None),
        P(("row", "col"), None, None),
        P(("row", "col"), None, None),
        P(("row", "col"), None, None),
    )
    out_specs = (P(None, None, "row", "col"), P())
    return jax.shard_map(
        functools.partial(body, DIMS),
        mesh=mesh,
        in_specs=in_specs,
        out_specs=out_specs,
        check_vma=False,
    )
```

```python
import functools
import math

import jax
import jax.numpy as jnp
import numpy as np
from jax import lax
from jax.experimental import pallas as pl
from jax.experimental.pallas import tpu as pltpu
from jax.sharding import PartitionSpec as P

PROPAGATION = 0.5
OBJECT_RATE = 0.1
PROBE_RATE = 0.5
N = 256
HALF = 128
NBK = 16
DIMS = dict(yh=2, z=4, yl=2, x=4, core=2)
MESH = pl.DeviceIdType.MESH
PIECES = ((0, 0, 48, False), (0, 48, 208, False), (1, 0, 168, True))
LONG = (1, 168, 88)
N_SEMS = 96
GROUP = 2
F32 = jnp.float32
BF16 = jnp.bfloat16


def block_pairs():
    n = np.arange(N)
    dft = np.exp(-2j * np.pi * np.outer(n, n) / N) / math.sqrt(N)
    freq = np.where(n < HALF, n, n - N).astype(np.float64)
    chirp = np.exp(-1j * np.pi * PROPAGATION * freq * freq / N)
    prop = dft.conj().T @ (chirp[:, None] * dft)
    fu, fv = dft[0::2, :HALF], dft[1::2, :HALF]
    first, second = prop[:HALF, :HALF], prop[:HALF, HALF:]
    cu, cv = (first + second) / 2, (first - second) / 2
    return {
        "prop": (cu, cv),
        "dft": (fu, fv),
        "idft": (fu.conj().T, fv.conj().T),
        "adj": (cu.conj().T, cv.conj().T),
    }


ORDER = ("prop", "dft", "idft", "adj")


def tables():
    left, right = [], []
    pairs = block_pairs()
    for name in ORDER:
        for m in pairs[name]:
            real = np.block([[m.real, -m.imag], [m.imag, m.real]]).astype(np.float32)
            hi = np.asarray(real, dtype=jnp.bfloat16)
            lo = np.asarray(real - hi.astype(np.float32), dtype=jnp.bfloat16)
            left.append(np.concatenate([hi, hi, lo], 1))
            right.append(np.concatenate([hi.T, hi.T, lo.T], 0))
    return np.stack(left), np.stack(right)


def permutation():
    perm = np.zeros((N, N), np.float32)
    for p in range(N):
        perm[p, 2 * p if p < HALF else 2 * (p - HALF) + 1] = 1
    rows = np.asarray(perm, dtype=jnp.bfloat16)
    cols = np.asarray(perm.T, dtype=jnp.bfloat16)
    spread = np.zeros((NBK, N), np.float32)
    for p in range(N):
        spread[(p % HALF) // 8, p] = 1
    return rows, cols, spread


def split(x):
    hi = x.astype(BF16)
    lo = (x - hi.astype(F32)).astype(BF16)
    return hi, lo


def dot(a, b):
    return jnp.dot(a, b, preferred_element_type=F32)


def along_cols(re, im, right_ref, op, pre, post):
    a, b, c, d = re[:, :HALF], re[:, HALF:], im[:, :HALF], im[:, HALF:]
    if pre:
        u = jnp.concatenate([a + b, c + d], 1)
        v = jnp.concatenate([a - b, c - d], 1)
    else:
        u = jnp.concatenate([a, c], 1)
        v = jnp.concatenate([b, d], 1)
    out = []
    for i, x in enumerate((u, v)):
        hi, lo = split(x)
        out.append(dot(jnp.concatenate([hi, lo, hi], 1), right_ref[2 * op + i]))
    yu, yv = out
    if post:
        p, m = yu + yv, yu - yv
    else:
        p, m = yu, yv
    return (
        jnp.concatenate([p[:, :HALF], m[:, :HALF]], 1),
        jnp.concatenate([p[:, HALF:], m[:, HALF:]], 1),
    )


def along_rows(re, im, left_ref, op, pre, post):
    a, b, c, d = re[:HALF], re[HALF:], im[:HALF], im[HALF:]
    if pre:
        u = jnp.concatenate([a + b, c + d], 0)
        v = jnp.concatenate([a - b, c - d], 0)
    else:
        u = jnp.concatenate([a, c], 0)
        v = jnp.concatenate([b, d], 0)
    out = []
    for i, x in enumerate((u, v)):
        hi, lo = split(x)
        out.append(dot(left_ref[2 * op + i], jnp.concatenate([hi, lo, hi], 0)))
    yu, yv = out
    if post:
        p, m = yu + yv, yu - yv
    else:
        p, m = yu, yv
    return (
        jnp.concatenate([p[:HALF], m[:HALF]], 0),
        jnp.concatenate([p[HALF:], m[HALF:]], 0),
    )


def transform(re, im, left_ref, right_ref, op, pre, post):
    re, im = along_cols(re, im, right_ref, op, pre, post)
    return along_rows(re, im, left_ref, op, pre, post)


def transforms(waves, left_ref, right_ref, op, pre, post):
    waves = [along_cols(*w, right_ref, op, pre, post) for w in waves]
    return [along_rows(*w, left_ref, op, pre, post) for w in waves]


def complex_mul(a, b):
    return a[0] * b[0] - a[1] * b[1], a[0] * b[1] + a[1] * b[0]


def conj_mul(a, b):
    return a[0] * b[0] + a[1] * b[1], a[1] * b[0] - a[0] * b[1]


def kernel(
    batch,
    rate,
    dims,
    offset_hbm,
    trans_hbm,
    probe_hbm,
    frames_hbm,
    lower_hbm,
    span_hbm,
    left_hbm,
    right_hbm,
    perm_rows_hbm,
    perm_cols_hbm,
    spread_hbm,
    newtrans_hbm,
    newprobe_hbm,
    own0,
    own1,
    bel0,
    bel1,
    gown0,
    gown1,
    gbel0,
    gbel1,
    rin0,
    rin1,
    din0,
    din1,
    relay_up,
    relay_down,
    long_up,
    long_down,
    side_mid,
    offset_ref,
    frames,
    left,
    right,
    probe_ref,
    lower_ref,
    span_ref,
    perm_rows_ref,
    perm_cols_ref,
    spread_ref,
    meas,
    wav,
    patch0,
    amp,
    piece,
    gacc,
    gfull,
    stage_core,
    stage_plane,
    stage_z,
    local_sem,
    send_sem,
    recv_sem,
):
    own, bel = (own0, own1), (bel0, bel1)
    gown, gbel = (gown0, gown1), (gbel0, gbel1)
    rin, din = (rin0, rin1), (din0, din1)
    relay, longs = (relay_up, relay_down), (long_up, long_down)
    n_z, n_x, n_yl, n_yh = dims["z"], dims["x"], dims["yl"], dims["yh"]
    n_core = dims["core"]
    n_row, n_col = n_yh * n_z, n_yl * n_x * n_core
    row, col = lax.axis_index("row"), lax.axis_index("col")
    yh, z = row // n_z, row % n_z
    yl, x, core = col // (n_core * n_x), (col // n_core) % n_x, col % n_core
    y_digit = yh * n_yl + yl
    n_y = n_yh * n_yl

    has_up, has_down = row > 0, row < n_row - 1
    has_left, has_right = col > 0, col < n_col - 1
    up, down = (row - 1, col), (row + 1, col)
    lft, rgt = (row, col - 1), (row, col + 1)

    turn = n_x * n_core

    def core_member(m):
        return (row, (yl * n_x + x) * n_core + m)

    def plane_member(m):
        y, x = m // n_x, m % n_x
        return ((y // n_yl) * n_z + z, ((y % n_yl) * n_x + x) * n_core + core)

    def z_member(m):
        return (yh * n_z + m, col)

    numbers = {}

    def number(*key):
        return numbers.setdefault(key, len(numbers))

    def load(src, dst, i):
        return pltpu.make_async_copy(src, dst, local_sem.at[i])

    loads = []
    for s in range(2):
        for c in range(2):
            loads.append(
                load(trans_hbm.at[s, :, :, pl.ds(c * N, N)], own[s].at[c], 2 * s + c)
            )
    for src, dst in (
        (offset_hbm, offset_ref),
        (frames_hbm, frames),
        (probe_hbm, probe_ref),
        (lower_hbm, lower_ref),
        (span_hbm, span_ref),
        (perm_rows_hbm, perm_rows_ref),
        (perm_cols_hbm, perm_cols_ref),
        (spread_hbm, spread_ref),
        (left_hbm, left),
        (right_hbm, right),
    ):
        loads.append(load(src, dst, len(loads)))

    barrier = pltpu.get_barrier_semaphore()

    def hail(dev):
        pl.semaphore_signal(barrier, inc=1, device_id=dev, device_id_type=MESH)

    for cond, dev in (
        (has_up, up),
        (has_down, down),
        (has_left, lft),
        (has_right, rgt),
    ):

        @pl.when(cond)
        def _(dev=dev):
            hail(dev)

    groups = (
        (core_member, n_core, core),
        (plane_member, n_y * n_x, y_digit * n_x + x),
        (z_member, n_z, z),
    )
    for member, size, me in groups:
        for k in range(1, size):
            hail(member((me + k) % size))
    hails = sum(size - 1 for _, size, _ in groups)
    for cond in (has_up, has_down, has_left, has_right):
        hails = hails + jnp.where(cond, 1, 0)
    edges = ()
    if n_yh > 1:
        edges = (
            (row, n_z + 2, (n_z - 1, col)),
            (row, n_z - 1, (n_z + 2, col)),
            (row, 1, (n_z, col)),
            (row, n_z, (1, col)),
        )
    if n_yl > 1:
        edges += (
            (col, 0, (row, turn - 1)),
            (col, turn - 1, (row, 0)),
            (col, n_col - 1, (row, turn)),
            (col, turn, (row, n_col - 1)),
        )
    for at, here, there in edges:

        @pl.when(at == here)
        def _(there=there):
            hail(there)

        hails = hails + jnp.where(at == here, 1, 0)
    pl.semaphore_wait(barrier, hails)

    def remote(src, dst, key, dev):
        i = number(*key)
        return pltpu.make_async_remote_copy(
            src_ref=src,
            dst_ref=dst,
            send_sem=send_sem.at[i],
            recv_sem=recv_sem.at[i],
            device_id=dev,
            device_id_type=MESH,
        )

    def on(cond, f):
        @pl.when(cond)
        def _():
            f()

    def both(*conds):
        return functools.reduce(jnp.logical_and, conds)

    n_pieces = len(PIECES)
    split_rows = n_yh > 1

    class Halo:
        def __init__(self, way, s):
            self.way, self.s = way, s
            self.sends, self.takes = (has_up, has_down) if way < 0 else (has_down, has_up)
            self.next = (row + way, col)
            self.edge = n_z if way < 0 else n_z - 1
            self.relay = n_row - 1 if way < 0 else 0
            self.last = self.edge + way
            self.ring = (yh * n_z + (z - way + n_z) % n_z, col)
            self.from1 = yh * n_z + (z + way + n_z) % n_z
            self.from2 = yh * n_z + (z + 2 * way + n_z) % n_z
            none = 0 if way < 0 else n_row - 1
            self.pass1 = jnp.logical_and(n_z > 2, self.from1 != none)
            self.pass2 = jnp.logical_and(n_z > 2, self.from2 != none)

        def ends(self, half, start, rows):
            here = pl.ds(start, rows)
            if self.way < 0:
                src = trans_hbm.at[self.s, :, here, pl.ds(half * N, N)]
                return src, bel[self.s].at[half, :, here]
            return gbel[self.s].at[half, :, here], din[self.s].at[half, :, here]

        def piece(self, k):
            half, start, rows, _ = PIECES[k]
            src, dst = self.ends(half, start, rows)
            return remote(src, dst, ("piece", self.way, self.s, k), self.next)

        def middle(self, k):
            first = sum(p[2] for p in PIECES[:k] if p[3])
            return relay[max(self.way, 0)].at[self.s, :, pl.ds(first, PIECES[k][2])]

        def first_leg(self, k):
            half, start, rows, _ = PIECES[k]
            src, _ = self.ends(half, start, rows)
            mid = self.middle(k)
            return remote(src, mid, ("leg", self.way, self.s, k), (self.relay, col))

        def second_leg(self, k):
            half, start, rows, _ = PIECES[k]
            _, dst = self.ends(half, start, rows)
            mid = self.middle(k)
            return remote(mid, dst, ("piece", self.way, self.s, k), (self.last, col))

        def relayed(self, k):
            return split_rows and PIECES[k][3]

        def start_piece(self, k):
            if not self.relayed(k):
                on(self.sends, self.piece(k).start)
            else:
                on(both(self.sends, row != self.edge), self.piece(k).start)

        def start_legs(self):
            for k in range(n_pieces):
                if self.relayed(k):
                    on(row == self.edge, self.first_leg(k).start)

        def pass_on(self):
            for k in range(n_pieces):
                if self.relayed(k):

                    @pl.when(row == self.relay)
                    def _(k=k):
                        self.first_leg(k).wait_recv()
                        self.second_leg(k).start()

        def wait_piece(self, k):
            on(self.takes, self.piece(k).wait_recv)

        def hop(self, h):
            src, dst = self.ends(*LONG)
            mids = longs[max(self.way, 0)]
            src = src if h == 0 else mids.at[self.s, h - 1]
            dst = dst if h == 2 else mids.at[self.s, h]
            dev = (self.from2 + self.way, col) if h == 2 else self.ring
            return remote(src, dst, ("long", self.way, self.s, h), dev)

        def start_long(self):
            on(self.sends, self.hop(0).start)

        def pass_long(self, h):
            @pl.when((self.pass1, self.pass2)[h])
            def _():
                self.hop(h).wait_recv()
                self.hop(h + 1).start()

        def wait_long(self):
            on(self.takes, self.hop(2).wait_recv)

        def finish(self):
            for k in range(n_pieces):
                if not self.relayed(k):
                    on(self.sends, self.piece(k).wait_send)
                    continue
                on(both(self.sends, row != self.edge), self.piece(k).wait_send)
                on(row == self.edge, self.first_leg(k).wait_send)
                on(row == self.relay, self.second_leg(k).wait_send)
            on(self.sends, self.hop(0).wait_send)
            on(self.pass1, self.hop(1).wait_send)
            on(self.pass2, self.hop(2).wait_send)

    fwd = Halo(-1, 0), Halo(-1, 1)
    back = Halo(1, 0), Halo(1, 1)

    class Side:
        def __init__(self, way, s):
            self.way, self.s = way, s
            self.sends, self.takes = (has_left, has_right) if way < 0 else (has_right, has_left)
            self.edge = turn if way < 0 else turn - 1
            self.relay = 0 if way < 0 else n_col - 1
            self.mid = side_mid.at[max(way, 0), s]
            if way < 0:
                self.src, self.dst = trans_hbm.at[s, :, :, pl.ds(0, N)], own[s].at[2]
            else:
                self.src, self.dst = gown[s].at[2], rin[s].at[0]
            self.relayed = n_yl > 1

        def whole(self):
            return remote(self.src, self.dst, ("side", self.way, self.s), (row, col + self.way))

        def first_leg(self):
            return remote(self.src, self.mid, ("side_leg", self.way, self.s), (row, self.relay))

        def second_leg(self):
            there = (row, self.edge + self.way)
            return remote(self.mid, self.dst, ("side", self.way, self.s), there)

        def start(self):
            if not self.relayed:
                on(self.sends, self.whole().start)
            else:
                on(both(self.sends, col != self.edge), self.whole().start)

        def start_leg(self):
            if self.relayed:
                on(col == self.edge, self.first_leg().start)

        def pass_on(self):
            if self.relayed:

                @pl.when(col == self.relay)
                def _():
                    self.first_leg().wait_recv()
                    self.second_leg().start()

        def wait(self):
            on(self.takes, self.whole().wait_recv)

        def finish(self):
            if not self.relayed:
                on(self.sends, self.whole().wait_send)
                return
            on(both(self.sends, col != self.edge), self.whole().wait_send)
            on(col == self.edge, self.first_leg().wait_send)
            on(col == self.relay, self.second_leg().wait_send)

    fwd_side = Side(-1, 0), Side(-1, 1)
    back_side = Side(1, 0), Side(1, 1)

    def fwd_corner(s):
        return remote(bel[s].at[0], bel[s].at[2], ("fwd_corner", s), lft)

    def back_corner(s):
        return remote(gbel[s].at[2], rin[s].at[1], ("back_corner", s), rgt)

    late = [k for k in range(n_pieces) if PIECES[k][0] == 0]
    early = [k for k in range(n_pieces) if PIECES[k][0] == 1]

    fwd[0].start_long()
    fwd[0].start_legs()
    for k in late + early:
        fwd[0].start_piece(k)
    fwd_side[0].start_leg()
    fwd_side[0].start()

    for c in loads:
        c.start()

    zero3 = jnp.zeros((2, N, N), F32)
    for s in range(2):

        @pl.when(jnp.logical_not(has_down))
        def _(s=s):
            for c in range(3):
                bel[s][c] = zero3

        @pl.when(jnp.logical_not(has_right))
        def _(s=s):
            own[s][2] = zero3
            on(has_down, functools.partial(bel[s].__setitem__, 2, zero3))

        @pl.when(jnp.logical_not(has_up))
        def _(s=s):
            for c in range(2):
                din[s][c] = zero3

        @pl.when(jnp.logical_not(has_left))
        def _(s=s):
            for c in range(2):
                rin[s][c] = zero3

    for c in loads[4:]:
        c.wait()

    def place(j):
        return offset_ref[0, j] & (N - 1), offset_ref[1, j] & (2 * N - 1)

    @pl.loop(0, batch)
    def _(j):
        counts = frames[j].astype(F32).astype(BF16)
        mixed = dot(perm_rows_ref[...], counts).astype(BF16)
        counts = dot(mixed, perm_cols_ref[...])
        base = 0.02 * jnp.exp2(lower_ref[j].astype(F32) * 0.25)
        extent = (0.1 / 255.0) * jnp.exp2(span_ref[j].astype(F32) * 0.25)

        def widen(small):
            wide = jnp.dot(
                small,
                spread_ref[...],
                precision=lax.Precision.HIGHEST,
                preferred_element_type=F32,
            )
            tall = jnp.broadcast_to(wide[:, None, :], (NBK, 8, N)).reshape(HALF, N)
            return jnp.concatenate([tall, tall], 0)

        meas[j] = widen(base) + counts * widen(extent)
        y, x = place(j)
        shift = x % N
        for p in range(2):
            wav[j, p] = pltpu.roll(pltpu.roll(probe_ref[p], shift, 1), y, 0)

    def masks(j):
        y, x = place(j)
        rows = lax.broadcasted_iota(jnp.int32, (N, N), 0) >= y
        cols = lax.broadcasted_iota(jnp.int32, (N, N), 1) >= x % N
        return rows, cols, x // N

    def take(s, j, p):
        rows, cols, k = masks(j)
        here = jnp.where(cols, own[s][k, p], own[s][k + 1, p])
        below = jnp.where(cols, bel[s][k, p], bel[s][k + 1, p])
        return jnp.where(rows, here, below)

    def arrive(s):
        for k in late:
            fwd[s].wait_piece(k)
        on(both(has_down, has_left), fwd_corner(s).start)
        fwd[s].pass_on()
        for k in early:
            fwd[s].wait_piece(k)
        fwd[s].wait_long()
        fwd_side[s].wait()
        on(both(has_down, has_right), fwd_corner(s).wait_recv)

    fwd[0].pass_long(0)
    fwd[1].start_long()
    fwd[1].start_legs()
    for k in late + early:
        fwd[1].start_piece(k)
    fwd_side[1].start_leg()
    fwd_side[1].start()
    fwd_side[0].pass_on()
    fwd[0].pass_long(1)
    fwd[1].pass_long(0)
    fwd_side[1].pass_on()
    for c in loads[:4]:
        c.wait()
    arrive(0)

    @pl.loop(0, batch)
    def _(j):
        patch = take(0, j, 0), take(0, j, 1)
        patch0[j, 0], patch0[j, 1] = patch
        wave = complex_mul((wav[j, 0], wav[j, 1]), patch)
        amp[j, 0], amp[j, 1] = transform(*wave, left, right, 0, True, True)

    fwd[1].pass_long(1)
    arrive(1)

    @pl.loop(0, batch // GROUP)
    def _(i):
        js = [GROUP * i + k for k in range(GROUP)]
        patches = [(take(1, j, 0), take(1, j, 1)) for j in js]
        incoming = [(amp[j, 0], amp[j, 1]) for j in js]
        far = [complex_mul(a, t) for a, t in zip(incoming, patches)]
        far = transforms(far, left, right, 1, True, False)
        misfit = [re * re + im * im - meas[j] for (re, im), j in zip(far, js)]
        waves = [(m * re, m * im) for m, (re, im) in zip(misfit, far)]
        waves = transforms(waves, left, right, 2, False, True)
        for j, wave, a, t in zip(js, waves, incoming, patches):
            piece[j, 0], piece[j, 1] = conj_mul(wave, a)
            amp[j, 0], amp[j, 1] = conj_mul(wave, t)

    def accumulate(s, below):
        total = gbel[s] if below else gown[s]

        @pl.loop(0, N // 8)
        def _(i):
            here = pl.ds(pl.multiple_of(i * 8, 8), 8)
            rows = lax.broadcasted_iota(jnp.int32, (8, N), 0) + i * 8
            cols = lax.broadcasted_iota(jnp.int32, (8, N), 1)
            sums = [[jnp.zeros((8, N), F32) for _ in range(3)] for _ in range(2)]
            for j in range(batch):
                y, x = place(j)
                inside = rows < y if below else rows >= y
                target = x // N + jnp.where(cols >= x % N, 0, 1)
                target = jnp.where(inside, target, 3)
                for c in range(3):
                    there = target == c
                    for p in range(2):
                        sums[p][c] += jnp.where(there, piece[j, p, here, :], 0.0)
            for p in range(2):
                for c in range(3):
                    total[c, p, here, :] = sums[p][c]

    def send_back_late(s):
        @pl.when(both(has_left, has_down))
        def _():
            back_corner(s).wait_recv()
            gbel[s][0] += rin[s][1]

        back[s].start_piece(late[0])

    def send_back_last(s):
        for k in late[1:]:
            back[s].start_piece(k)

    accumulate(1, True)
    on(both(has_right, has_down), back_corner(1).start)
    back[1].start_long()
    back[1].start_legs()
    for k in early:
        back[1].start_piece(k)
    accumulate(1, False)
    back_side[1].start_leg()
    back_side[1].start()

    gacc[...] = jnp.zeros_like(gacc)

    @pl.loop(0, batch // GROUP)
    def _(i):
        on(i == batch // GROUP - 1, lambda: back[1].pass_long(0))
        js = [GROUP * i + k for k in range(GROUP)]
        waves = [(amp[j, 0], amp[j, 1]) for j in js]
        first = [(wav[j, 0], wav[j, 1]) for j in js]
        patches = [(patch0[j, 0], patch0[j, 1]) for j in js]
        waves = transforms(waves, left, right, 3, True, True)
        terms = [conj_mul(w, t) for w, t in zip(waves, patches)]
        grads = [conj_mul(w, a) for w, a in zip(waves, first)]
        for p in range(2):
            turned = 0.0
            for j, term in zip(js, terms):
                y, x = place(j)
                turned += pltpu.roll(pltpu.roll(term[p], (N - y) % N, 0), (N - x % N) % N, 1)
            for h in range(2):
                gacc[pl.ds((2 * p + h) * N, N), :] += turned[:, h * HALF : (h + 1) * HALF]
        for j, grad in zip(js, grads):
            piece[j, 0], piece[j, 1] = grad

    send_back_late(1)
    send_back_last(1)

    chunks = [gacc.shape[0]]
    for _, size, _ in groups[:2]:
        chunks.append(chunks[-1] // size)
    starts = [0]
    for chunk, (_, _, me) in zip(chunks[1:], groups):
        starts.append(starts[-1] + me * chunk)
    stages = stage_core, stage_plane

    def part(ref, start, chunk):
        return ref.at[pl.ds(pl.multiple_of(start, 8), chunk), :]

    def scatter_start(g):
        member, size, me = groups[g]
        copies = []
        for k in range(1, size):
            m = (me + k) % size
            src = part(gacc, starts[g] + m * chunks[g + 1], chunks[g + 1])
            copies.append(remote(src, stages[g].at[k - 1], ("sum", g, k), member(m)))
        for c in copies:
            c.start()
        return copies

    def scatter_finish(g, copies):
        for c in copies:
            c.wait()
        mine = part(gacc, starts[g + 1], chunks[g + 1])
        got = mine[...]
        for k in range(1, groups[g][1]):
            got = got + stages[g][k - 1]
        mine[...] = got

    def gather_start(g):
        member, size, me = groups[g]
        held = part(gfull, starts[g + 1], chunks[g + 1])
        copies = [
            remote(held, held, ("whole", g, k), member((me + k) % size))
            for k in range(1, size)
        ]
        for c in copies:
            c.start()
        return copies

    def gather_finish(g, copies):
        member, size, me = groups[g]
        for k, c in enumerate(copies, 1):
            c.wait_send()
            m = (me - k + size) % size
            there = part(gfull, starts[g] + m * chunks[g + 1], chunks[g + 1])
            remote(there, there, ("whole", g, k), member(m)).wait_recv()

    stores = []

    def finish_tile(s):
        for c in (1, 0):
            for k in late if c == 0 else early:
                back[s].wait_piece(k)
            if c == 0:
                back_side[s].wait()
            else:
                back[s].wait_long()
            for p in range(2):
                value = gown[s][c, p] + din[s][c, p]
                if c == 0:
                    value = value + rin[s][0, p]
                own[s][c, p] = own[s][c, p] - OBJECT_RATE * value
            dst = newtrans_hbm.at[s, :, :, pl.ds(c * N, N)]
            stores.append(load(own[s].at[c], dst, len(stores)))
            stores[-1].start()

    copies = scatter_start(0)
    accumulate(0, True)
    for k in early:
        back[0].start_piece(k)
    back[0].start_legs()
    scatter_finish(0, copies)
    copies = scatter_start(1)
    on(both(has_right, has_down), back_corner(0).start)
    back[1].pass_long(1)
    back[0].start_long()
    back[1].pass_on()
    accumulate(0, False)
    back_side[0].start_leg()
    back_side[0].start()
    back_side[1].pass_on()
    send_back_late(0)
    back[0].pass_long(0)
    back[0].pass_on()
    scatter_finish(1, copies)

    mine = part(gacc, starts[2], chunks[2])
    copies = [
        remote(mine, stage_z.at[z], ("sum", 3, k), z_member((z + k) % n_z))
        for k in range(1, n_z)
    ]
    for c in copies:
        c.start()
    stage_z[z] = mine[...]
    send_back_last(0)
    for c in copies:
        c.wait()
    got = stage_z[0]
    for m in range(1, n_z):
        got = got + stage_z[m]
    part(gfull, starts[2], chunks[2])[...] = got

    copies = gather_start(1)
    back[0].pass_long(1)
    back_side[0].pass_on()
    gather_finish(1, copies)
    copies = gather_start(0)
    finish_tile(1)
    gather_finish(0, copies)

    for p in range(2):
        for h in range(2):
            cols = pl.ds(h * HALF, HALF)
            summed = gfull[pl.ds((2 * p + h) * N, N), :]
            probe_ref[p, :, cols] = probe_ref[p, :, cols] - rate * summed
    stores.append(load(probe_ref, newprobe_hbm, len(stores)))
    stores[-1].start()

    finish_tile(0)
    for c in stores:
        c.wait()

    for s in range(2):
        fwd[s].finish()
        back[s].finish()
        fwd_side[s].finish()
        on(both(has_down, has_left), fwd_corner(s).wait_send)
        on(both(has_right, has_down), back_corner(s).wait_send)
        back_side[s].finish()
    assert len(numbers) <= N_SEMS


def hand_on(trans, probe, out_trans, out_probe, held, held_probe, sems):
    pieces = [(probe.at[p], held_probe.at[p], out_probe.at[p]) for p in range(2)]
    for s in range(2):
        for p in range(2):
            for k in range(2):
                at = s, p, pl.ds(k * HALF, HALF)
                pieces.append((trans.at[at], held.at[at], out_trans.at[at]))
    takes, gives = [], []
    for i, (src, mid, dst) in enumerate(pieces):
        takes.append(pltpu.make_async_copy(src, mid, sems.at[0, i]))
        gives.append(pltpu.make_async_copy(mid, dst, sems.at[1, i]))
    for take in takes:
        take.start()
    for take, give in zip(takes, gives):
        take.wait()
        give.start()
    for give in gives:
        give.wait()


def body(dims, transmission, probe, offsets, frames, lower_level, level_span):
    batch = offsets.shape[0]
    left, right = tables()
    perm_rows, perm_cols, spread = permutation()
    n_y = dims["yh"] * dims["yl"]
    total = 2 * 2 * N
    chunk_core = total // dims["core"]
    members = n_y * dims["x"]
    chunk_plane = chunk_core // members
    count_all = batch * lax.axis_size("row") * lax.axis_size("col")
    rate = PROBE_RATE / math.sqrt(count_all)
    any_space = pl.BlockSpec(memory_space=pl.ANY)

    def block(*shape, dtype=F32):
        return pltpu.VMEM(shape, dtype)

    tile = [block(3, 2, N, N) for _ in range(8)]
    arriving = [block(2, 2, N, N) for _ in range(4)]
    scratch = (
        tile
        + arriving
        + [block(2, 2, sum(p[2] for p in PIECES if p[3]), N) for _ in range(2)]
        + [block(2, 2, 2, LONG[2], N) for _ in range(2)]
        + [block(2, 2, 2, N, N)]
        + [
            pltpu.SMEM((2, batch), jnp.int32),
            block(batch, N, N, dtype=jnp.int32),
            block(8, N, 3 * N, dtype=BF16),
            block(8, 3 * N, N, dtype=BF16),
            block(2, N, N),
            block(batch, NBK, NBK, dtype=jnp.int32),
            block(batch, NBK, NBK, dtype=jnp.int32),
            block(N, N, dtype=BF16),
            block(N, N, dtype=BF16),
            block(NBK, N),
            block(batch, N, N),
            block(batch, 2, N, N),
            block(batch, 2, N, N),
            block(batch, 2, N, N),
            block(batch, 2, N, N),
            block(total, HALF),
            block(total, HALF),
            block(1, chunk_core, HALF),
            block(max(members - 1, 1), chunk_plane, HALF),
            block(dims["z"], chunk_plane, HALF),
            pltpu.SemaphoreType.DMA((14,)),
            pltpu.SemaphoreType.DMA((N_SEMS,)),
            pltpu.SemaphoreType.DMA((N_SEMS,)),
        ]
    )
    results = pl.pallas_call(
        functools.partial(kernel, batch, rate, dims),
        out_shape=(
            jax.ShapeDtypeStruct(transmission.shape, F32),
            jax.ShapeDtypeStruct(probe.shape, F32),
        ),
        in_specs=[any_space] * 11,
        out_specs=(any_space, any_space),
        scratch_shapes=scratch,
        compiler_params=pltpu.CompilerParams(
            collective_id=0, has_side_effects=True, vmem_limit_bytes=62 * 2**20
        ),
        name="ptycho_step",
    )(
        offsets.T,
        transmission,
        probe,
        frames,
        lower_level,
        level_span,
        left,
        right,
        perm_rows,
        perm_cols,
        spread,
    )
    return pl.pallas_call(
        hand_on,
        out_shape=tuple(jax.ShapeDtypeStruct(r.shape, r.dtype) for r in results),
        in_specs=[any_space] * 2,
        out_specs=(any_space, any_space),
        scratch_shapes=[
            block(*transmission.shape),
            block(*probe.shape),
            pltpu.SemaphoreType.DMA((2, 10)),
        ],
        name="hand_on",
    )(*results)


def solution(mesh):
    in_specs = (
        P(None, None, "row", "col"),
        P(),
        P(("row", "col"), None),
        P(("row", "col"), None, None),
        P(("row", "col"), None, None),
        P(("row", "col"), None, None),
    )
    out_specs = (P(None, None, "row", "col"), P())
    return jax.shard_map(
        functools.partial(body, DIMS),
        mesh=mesh,
        in_specs=in_specs,
        out_specs=out_specs,
        check_vma=False,
    )
```
